256 devices in a mesh: gx: 8 (over x, core), gy: 8 (over z_lo, y), pair: 4 (over z_hi).
Axes of the slice: x: 4, y: 4, z: 8 (z_hi: 4, z_lo: 2; z = z_hi * 2 + z_lo), core: 2. Of those that a mesh axis runs over, the one named last changes fastest.
Arguments:
- features: bfloat16 [8, 8, 4, 8, 32, 512], P('gx', 'gy', 'pair'), may hold values from -6 to 6
- cotangent: bfloat16 [8, 8, 4, 8, 32, 512], P('gx', 'gy', 'pair'), may hold values from -6 to 6
- masks: int32 [8, 8, 4, 8, 512], P('gx', 'gy', 'pair'), may hold values 0 or 1
- coords: int32 [8, 8, 4, 3, 8], P('gx', 'gy', 'pair'), may hold values from 0 to 3, as said below
- counts: int32 [8, 8, 4], P('gx', 'gy', 'pair'), may hold values from 2 to 8, as said below
- weight: bfloat16 [864, 32], replicated, may hold values from -0.21875 to 0.21875
- bias: float32 [32], replicated, may hold values from -3 to 3
Outputs:
- output: bfloat16 [8, 8, 4, 8, 32, 512], P('gx', 'gy', 'pair')
- grad_input: bfloat16 [8, 8, 4, 8, 32, 512], P('gx', 'gy', 'pair')
- grad_weight: float32 [864, 32], replicated
- grad_bias: float32 [32], replicated
The draws below stay inside these ranges and needn't reach their ends.
Inputs may be any that keep to these rules, and one draw needn't show every extreme that they name: `coords`: all 8 slots of a device name distinct tiles of its brick: component 0 lies below 4, component 1 below 4, component 2 below 2. A device's active tiles fill its slots 0 to counts - 1. Among the devices that differ only in their pair index, exactly half hold more than 4 tiles and the others at most 4; every draw has a device with 8 tiles and one with 4.
All inputs are finite; a program needn't handle non-finite values. No bound on the sum of `masks` on one device may be relied on, other than what follows from the above.
Results may differ from the reference program's by a relative error of at most 0.0035.
Values may be sent and summed in bfloat16 or wider, within the bound.
No kernel may reach another device: no remote copies, remote signals or barrier semaphores. Data moves between devices by JAX's collectives and lax.ppermute only.
A program may use at most 192 MiB of HBM per device.

```python
import math
import jax
import jax.numpy as jnp
from jax import lax

C = 32
TILE = 8
TX = 4
TY = 4
TZ = 2
SLOTS = 8
N_GX = 8
N_GY = 8
N_PAIR = 4


def draw_coords(key, part):
    key = jax.random.fold_in(key, 11)
    positions_all = TX * TY * TZ
    devices = N_GX * N_GY * N_PAIR
    device_keys = jax.random.split(key, devices)
    chosen = jax.vmap(lambda single: jax.random.permutation(single, positions_all)[:SLOTS])(device_keys).astype(jnp.int32)
    along_x = chosen // (TY * TZ)
    along_y = chosen // TZ % TY
    along_z = chosen % TZ
    return jnp.stack([along_x, along_y, along_z], axis=1).reshape(N_GX, N_GY, N_PAIR, 3, SLOTS).astype(jnp.int32)


def draw_counts(key, part):
    key = jax.random.fold_in(key, 23)
    first_key, second_key, third_key = jax.random.split(key, 3)
    groups = N_GX * N_GY
    orders = jax.vmap(lambda single: jax.random.permutation(single, N_PAIR))(jax.random.split(first_key, groups))
    heavy_flags = orders < N_PAIR // 2
    upper_loads = jax.random.randint(second_key, (groups, N_PAIR), 3 * SLOTS // 4 + 1, SLOTS + 1)
    lower_loads = jax.random.randint(third_key, (groups, N_PAIR), SLOTS // 4, SLOTS // 2 + 1)
    tile_loads = jnp.where(heavy_flags, upper_loads, lower_loads)
    tile_loads = tile_loads.at[0].set(jnp.where(heavy_flags[0], SLOTS, SLOTS // 2))
    return tile_loads.reshape(N_GX, N_GY, N_PAIR).astype(jnp.int32)


def place_ends(array, key, least, high):
    place = [jax.random.randint(jax.random.fold_in(key, axis), (), 0, length) for axis, length in enumerate(array.shape)]
    main_axis = array.shape.index(max(array.shape))
    beside = place[:main_axis] + [(place[main_axis] + 1) % array.shape[main_axis]] + place[main_axis + 1:]
    return array.at[tuple(place)].set(least).at[tuple(beside)].set(high)


def block_levels(key, extent, cuts, low, largest):
    def one(axis_at, blocks):
        heights = jax.random.uniform(jax.random.fold_in(jax.random.fold_in(key, 6), axis_at), (blocks,), jnp.float32, low / len(cuts), largest / len(cuts))
        return jnp.repeat(jnp.exp(heights), extent[axis_at] // blocks).reshape((-1,) + (1,) * (len(extent) - axis_at - 1))

    level = one(*cuts[0])
    for cut in cuts[1:]:
        level = level * one(*cut)
    return level


def centred(key, dims, deviation, reach, cuts=(), kind=jnp.bfloat16):
    loudness = block_levels(key, dims, cuts, -0.22, 0.18) if cuts else 1.0
    array = jax.random.normal(key, dims, jnp.float32) * deviation * loudness
    return jnp.minimum(jnp.maximum(array, -reach), reach).astype(kind)


def setup_inputs(seed: int = 0) -> dict:
    keys = jax.random.split(jax.random.key(seed), 8)
    features = centred(keys[0], (N_GX, N_GY, N_PAIR, SLOTS, C, TILE * TILE * TILE), 1.0, 6.0, ((0, 8), (1, 8), (2, 4)))
    cotangent = centred(keys[1], (N_GX, N_GY, N_PAIR, SLOTS, C, TILE * TILE * TILE), 1.0, 6.0, ((0, 8), (1, 8), (2, 4)))
    masks = place_ends((jax.random.randint(keys[2], (N_GX, N_GY, N_PAIR, SLOTS, TILE * TILE * TILE), 0, 2) < 1).astype(jnp.int32), jax.random.fold_in(keys[2], 1), 0, 1)
    coords = draw_coords(jax.random.fold_in(keys[7], 71), 0)
    counts = draw_counts(jax.random.fold_in(keys[7], 71), 0)
    weight = centred(keys[5], (27 * C, C), (27 * C) ** -0.5, 0.21875)
    bias = centred(keys[6], (C,), 0.5, 3.0, (), jnp.float32)
    return dict(features=features, cotangent=cotangent, masks=masks, coords=coords, counts=counts, weight=weight, bias=bias)


def face_views(tile_rows):
    layer_spans = (slice(7, 8), slice(0, 8), slice(0, 1))
    zero_row = jnp.zeros((1,) + tile_rows.shape[1:], tile_rows.dtype)
    extended = jnp.concatenate([tile_rows, zero_row], axis=0)
    face_list = []
    for along_x in range(3):
        for along_y in range(3):
            for along_z in range(3):
                face_list.append(extended[:, :, layer_spans[along_x], layer_spans[along_y], layer_spans[along_z]])
    return face_list

def neighbour_table(coords, counts):
    slot_index = jnp.arange(SLOTS, dtype=jnp.int32)
    brick_x = jnp.arange(N_GX, dtype=jnp.int32)[:, None, None, None]
    brick_y = jnp.arange(N_GY, dtype=jnp.int32)[None, :, None, None]
    sample = jnp.arange(N_PAIR, dtype=jnp.int32)[None, None, :, None]
    global_x = brick_x * TX + coords[:, :, :, 0, :]
    global_y = brick_y * TY + coords[:, :, :, 1, :]
    global_z = coords[:, :, :, 2, :]
    sample_ids = jnp.broadcast_to(sample, global_x.shape)
    row_ids = ((brick_x * N_GY + brick_y) * N_PAIR + sample) * SLOTS + slot_index
    row_ids = jnp.where(slot_index < counts[..., None], row_ids, -1).astype(jnp.int32)
    tile_map = jnp.full((N_PAIR, N_GX * TX + 2, N_GY * TY + 2, TZ + 2), -1, jnp.int32)
    tile_map = tile_map.at[sample_ids, global_x + 1, global_y + 1, global_z + 1].max(row_ids)
    columns = []
    for along_x in range(3):
        for along_y in range(3):
            for along_z in range(3):
                columns.append(tile_map[sample_ids, global_x + along_x, global_y + along_y, global_z + along_z])
    lookup = jnp.stack(columns, axis=-1)
    devices = N_GX * N_GY * N_PAIR
    lookup = jnp.where(lookup < 0, devices * SLOTS, lookup).astype(jnp.int32)
    return lookup.reshape(devices, SLOTS, 27)

def neighbourhoods(face_list, lookup):
    planes = []
    offset_id = 0
    for along_x in range(3):
        stack_y = []
        for along_y in range(3):
            pieces = []
            for along_z in range(3):
                pieces.append(jnp.take(face_list[offset_id], lookup[:, offset_id], axis=0))
                offset_id += 1
            stack_y.append(jnp.concatenate(pieces, axis=4))
        planes.append(jnp.concatenate(stack_y, axis=3))
    return jnp.concatenate(planes, axis=2)

def unfold(blocks):
    number, channels = (blocks.shape[0], blocks.shape[1])
    windows = []
    for offset_id in range(27):
        shift_x, shift_y, shift_z = (offset_id // 9, offset_id // 3 % 3, offset_id % 3)
        windows.append(blocks[:, :, shift_x:shift_x + 8, shift_y:shift_y + 8, shift_z:shift_z + 8])
    return jnp.stack(windows, axis=1).reshape(number, 27 * channels, 512)

def reference(features, cotangent, masks, coords, counts, weight, bias):
    devices = N_GX * N_GY * N_PAIR
    slot_index = jnp.arange(SLOTS, dtype=jnp.int32)
    active = (slot_index < counts[..., None]).astype(jnp.int32)
    live_mask = (masks * active[..., None]).astype(features.dtype)
    inputs = features * live_mask[:, :, :, :, None, :]
    grad_tiles = cotangent * live_mask[:, :, :, :, None, :]
    input_faces = face_views(inputs.reshape(devices * SLOTS, C, 8, 8, 8))
    grad_faces = face_views(grad_tiles.reshape(devices * SLOTS, C, 8, 8, 8))
    lookup = neighbour_table(coords, counts)
    flattened_weight = weight.astype(jnp.float32)
    reversed_kernel = flattened_weight.reshape(27, C, C)[::-1].transpose(0, 2, 1).reshape(27 * C, C)
    bias_column = bias.astype(jnp.float32)[None, :, None]

    def per_device(summed_weight, device_item):
        near_rows, local_gradients, own_live = device_item
        input_blocks = neighbourhoods(input_faces, near_rows).astype(jnp.float32)
        grad_blocks = neighbourhoods(grad_faces, near_rows).astype(jnp.float32)
        input_column_matrix = unfold(input_blocks)
        gradient_columns = unfold(grad_blocks)
        forward_pass = jnp.einsum('rzj,zs->rsj', input_column_matrix, flattened_weight)
        backward_pass = jnp.einsum('soy,oa->say', gradient_columns, reversed_kernel)
        summed_weight = summed_weight + jnp.einsum('upj,urj->pr', input_column_matrix, local_gradients.astype(jnp.float32))
        live_float = own_live.astype(jnp.float32)[:, None, :]
        result_out = (live_float * (forward_pass + bias_column)).astype(jnp.bfloat16)
        result_grad = (live_float * backward_pass).astype(jnp.bfloat16)
        return (summed_weight, (result_out, result_grad))
    own_all = grad_tiles.reshape(devices, SLOTS, C, 512)
    live_rows = live_mask.reshape(devices, SLOTS, 512)
    initial = jnp.zeros((27 * C, C), jnp.float32)
    summed_weight, (output, grad_input) = lax.scan(per_device, initial, (lookup, own_all, live_rows))
    norm_scale = 1.0 / math.sqrt(devices * SLOTS * 512)
    full_shape = (N_GX, N_GY, N_PAIR, SLOTS, C, 512)
    grad_bias = lax.optimization_barrier(jnp.sum(grad_tiles.astype(jnp.float32), axis=(0, 1, 2, 3, 5))) * norm_scale
    return (output.reshape(full_shape), grad_input.reshape(full_shape), summed_weight * norm_scale, grad_bias)
```

```python
import math

import jax
import jax.numpy as jnp
import numpy as np
from jax import lax
from jax.experimental import pallas as pl
from jax.experimental.pallas import tpu as pltpu
from jax.sharding import PartitionSpec as P

TX = 4
TY = 4
CH = 32
ROWS = 2 * CH
PLANES = 8 * TX + 2
SPAN = 10 * 128
KDIM = 9 * CH
GROWS = KDIM + 16
RED = 320


def face_matrix():
    m = np.zeros((512, 512), np.float32)
    for u in range(8):
        for c in range(8):
            m[64 * u + c, 16 * u + c] = 1
            m[64 * u + 56 + c, 128 + 16 * u + c] = 1
            m[8 * u + c, 256 + 16 * u + c] = 1
            m[448 + 8 * u + c, 384 + 16 * u + c] = 1
    return jnp.asarray(m, jnp.bfloat16)


def place_matrix():
    m = np.zeros((2, 128, 256), np.float32)
    for tz in range(2):
        for h in range(2):
            for b in range(8):
                for c in range(8):
                    m[tz, 64 * h + 8 * b + c, 128 * h + 16 * b + 8 * tz + c] = 1
    return jnp.asarray(m, jnp.bfloat16)


def window_matrix():
    m = np.zeros((2, 256, 128), np.float32)
    for tz in range(2):
        for y in range(10):
            for z in range(10):
                gz = 8 * tz - 1 + z
                if gz < 0 or gz > 15:
                    continue
                if y == 0:
                    source = 128 + 112 + gz
                elif y == 9:
                    source = 128 + gz
                else:
                    source = 16 * (y - 1) + gz
                m[tz, source, 10 * y + z] = 1
    return jnp.asarray(m, jnp.bfloat16)


def compact_matrix():
    m = np.zeros((256, 128), np.float32)
    for h in range(2):
        for b in range(8):
            for c in range(8):
                m[128 * h + 10 * b + c, 64 * h + 8 * b + c] = 1
    return jnp.asarray(m, jnp.bfloat16)


def dot(a, b):
    return lax.dot_general(a, b, (((1,), (0,)), ((), ())), preferred_element_type=jnp.float32)


def masked_tile(feat_ref, cot_ref, mask_ref, slot):
    live = mask_ref[pl.ds(slot, 1), :].astype(jnp.float32).astype(jnp.bfloat16)
    return jnp.concatenate([feat_ref[slot] * live, cot_ref[slot] * live], axis=0)


def faces_kernel(coords, counts, feat_ref, cot_ref, mask_ref, sel_ref, xlo_ref, xhi_ref, ylo_ref, yhi_ref):
    for ref in (xlo_ref, xhi_ref, ylo_ref, yhi_ref):
        ref[...] = jnp.zeros_like(ref)

    def body(slot, carry):
        tx, ty, tz = coords[0, slot], coords[1, slot], coords[2, slot]
        found = dot(masked_tile(feat_ref, cot_ref, mask_ref, slot), sel_ref[...])
        shift = 8 * tz

        def add(ref, place, block, on):
            @pl.when(on)
            def _():
                part = pltpu.roll(found[:, 128 * block : 128 * block + 128], shift, 1)
                ref[place] = ref[place] + part.astype(jnp.bfloat16)

        add(ylo_ref, tx, 0, ty == 0)
        add(yhi_ref, tx, 1, ty == TY - 1)
        add(xlo_ref, ty, 2, tx == 0)
        add(xhi_ref, ty, 3, tx == TX - 1)
        return carry

    lax.fori_loop(0, counts[0], body, 0)


def edges_kernel(left_ref, right_ref, ylo_ref, yhi_ref, lo_ref, hi_ref):
    lane = lax.broadcasted_iota(jnp.int32, (ROWS, 128), 1)
    lo_ref[0:TX] = ylo_ref[...]
    hi_ref[0:TX] = yhi_ref[...]

    def roll(value, shift):
        return pltpu.roll(value.astype(jnp.float32), shift, 1)

    lo = jnp.where(lane < 16, left_ref[0].astype(jnp.float32), roll(right_ref[0], 16))
    hi = jnp.where(lane < 16, roll(left_ref[TY - 1], 16), roll(right_ref[TY - 1], 32))
    lo_ref[TX] = lo.astype(jnp.bfloat16)
    hi_ref[TX] = hi.astype(jnp.bfloat16)


def main_kernel(
    coords, counts, feat_ref, cot_ref, mask_ref, left_ref, right_ref, lo_ref, hi_ref,
    wf_ref, wb_ref, bias_ref, place_ref, window_ref, compact_ref,
    out_ref, gin_ref, sums_ref, dense, columns, centre,
):
    dense[...] = jnp.zeros_like(dense)
    out_ref[...] = jnp.zeros_like(out_ref)
    gin_ref[...] = jnp.zeros_like(gin_ref)
    sums_ref[...] = jnp.zeros_like(sums_ref)
    centre[...] = jnp.zeros_like(centre)
    columns[0, KDIM:GROWS, :] = jnp.ones((GROWS - KDIM, SPAN), jnp.bfloat16)

    for ty in range(TY):
        dense[0, ty + 1] = left_ref[ty]
        dense[PLANES - 1, ty + 1] = right_ref[ty]
    for group in range(TX + 1):
        lo = lo_ref[group].astype(jnp.float32)
        hi = hi_ref[group].astype(jnp.float32)
        for j in range(8 if group < TX else 2):
            plane = 1 + 8 * group + j if group < TX else j * (PLANES - 1)
            dense[plane, 0] = pltpu.roll(lo, (112 - 16 * j) % 128, 1).astype(jnp.bfloat16)
            dense[plane, TY + 1] = pltpu.roll(hi, (128 - 16 * j) % 128, 1).astype(jnp.bfloat16)

    def place(slot, carry):
        tx, ty, tz = coords[0, slot], coords[1, slot], coords[2, slot]
        tile = masked_tile(feat_ref, cot_ref, mask_ref, slot)
        stacked = jnp.concatenate([tile[:, 128 * j : 128 * j + 128] for j in range(4)], axis=0)
        spread = dot(stacked, place_ref[tz]).astype(jnp.bfloat16)
        for a in range(8):
            j, h = a // 2, a % 2
            where = (1 + 8 * tx + a, 1 + ty)
            dense[where] = dense[where] + spread[ROWS * j : ROWS * j + ROWS, 128 * h : 128 * h + 128]
        return carry

    lax.fori_loop(0, counts[0], place, 0)

    lane = lax.broadcasted_iota(jnp.int32, (10, ROWS, 128), 2)
    column = lax.broadcasted_iota(jnp.int32, (CH, 128), 1)
    inside = jnp.where((column < 80) & (lax.rem(column, 10) < 8), 1.0, 0.0).astype(jnp.bfloat16)

    def work(slot, carry):
        tx, ty, tz = coords[0, slot], coords[1, slot], coords[2, slot]
        own = dense[pl.ds(8 * tx, 10), 1 + ty]
        below = dense[pl.ds(8 * tx, 10), ty]
        above = dense[pl.ds(8 * tx, 10), 2 + ty]
        zero = jnp.zeros_like(own)
        rim = jnp.where(lane >= 112, below, jnp.where(lane < 16, above, zero))
        both = jnp.concatenate([own.reshape(10 * ROWS, 128), rim.reshape(10 * ROWS, 128)], axis=1)
        windows = dot(both, window_ref[tz])
        for k in range(9):
            shift = (k // 3) * 10 + k % 3
            moved = windows if shift == 0 else pltpu.roll(windows, 128 - shift, 1)
            moved = moved.astype(jnp.bfloat16)
            for p in range(10):
                for f in range(2):
                    columns[f, CH * k : CH * k + CH, 128 * p : 128 * p + 128] = moved[
                        ROWS * p + CH * f : ROWS * p + CH * f + CH
                    ]
        for p in range(8):
            block = columns[1, 4 * CH : 5 * CH, 128 * (p + 1) : 128 * (p + 2)] * inside
            for dx in range(3):
                centre[CH * dx : CH * dx + CH, 128 * (p + dx) : 128 * (p + dx + 1)] = block
        sums_ref[0:GROWS] += lax.dot_general(
            columns[0], centre[...], (((1,), (1,)), ((), ())), preferred_element_type=jnp.float32
        )
        halves = []
        for f, w_ref in ((0, wf_ref), (1, wb_ref)):
            z = dot(w_ref[...], columns[f, 0:KDIM, :])
            y = z[0:CH, 0:1024] + z[CH : 2 * CH, 128:1152] + z[2 * CH : 3 * CH, 256:1280]
            if f == 0:
                y = y + bias_ref[:, 0:1]
            halves += [y[:, 256 * j : 256 * j + 256] for j in range(4)]
        packed = dot(jnp.concatenate(halves, axis=0).astype(jnp.bfloat16), compact_ref[...])
        live = mask_ref[pl.ds(slot, 1), :].astype(jnp.float32)
        for f, ref in ((0, out_ref), (1, gin_ref)):
            rows = [packed[CH * (4 * f + j) : CH * (4 * f + j) + CH] for j in range(4)]
            ref[slot] = (jnp.concatenate(rows, axis=1) * live).astype(jnp.bfloat16)
        return carry

    lax.fori_loop(0, counts[0], work, 0)


def shifted(axis, step):
    count = lax.axis_size(axis)
    return [(i, i + step) for i in range(count) if 0 <= i + step < count]


def exchange(block, axes):
    return lax.all_to_all(block, axes, 0, 0, tiled=True)


SMEM = pl.BlockSpec(memory_space=pltpu.SMEM)
VMEM = pl.BlockSpec(memory_space=pltpu.VMEM)


def kernel_weights(weight):
    w = weight.reshape(3, 9, CH, CH)
    forward = w.transpose(0, 3, 1, 2).reshape(3 * CH, KDIM)
    back = weight.reshape(27, CH, CH)[::-1].reshape(3, 9, CH, CH)
    backward = back.transpose(0, 2, 1, 3).reshape(3 * CH, KDIM)
    return forward, backward


def local(features, cotangent, masks, coords, counts, weight, bias):
    bf16, f32 = jnp.bfloat16, jnp.float32
    slots = features.shape[3]
    feat = features.reshape(slots, CH, 512)
    cot = cotangent.reshape(slots, CH, 512)
    mask = masks.reshape(slots, 512)
    coords = coords.reshape(3, slots)
    counts = counts.reshape(1)
    forward, backward = kernel_weights(weight)
    bias_wide = jnp.broadcast_to(bias[:, None], (CH, 128))

    face = jax.ShapeDtypeStruct((4, ROWS, 128), bf16)
    edge = jax.ShapeDtypeStruct((5, ROWS, 128), bf16)
    xlo, xhi, ylo, yhi = pl.pallas_call(
        faces_kernel,
        out_shape=[face] * 4,
        in_specs=[SMEM] * 2 + [VMEM] * 4,
        out_specs=[VMEM] * 4,
    )(coords, counts, feat, cot, mask, face_matrix())
    left = lax.ppermute(xhi, "gx", shifted("gx", 1))
    right = lax.ppermute(xlo, "gx", shifted("gx", -1))
    lo_send, hi_send = pl.pallas_call(
        edges_kernel,
        out_shape=[edge] * 2,
        in_specs=[VMEM] * 4,
        out_specs=[VMEM] * 2,
    )(left, right, ylo, yhi)
    low = lax.ppermute(hi_send, "gy", shifted("gy", 1))
    high = lax.ppermute(lo_send, "gy", shifted("gy", -1))

    out, gin, sums = pl.pallas_call(
        main_kernel,
        out_shape=[
            jax.ShapeDtypeStruct((slots, CH, 512), bf16),
            jax.ShapeDtypeStruct((slots, CH, 512), bf16),
            jax.ShapeDtypeStruct((RED, 128), f32),
        ],
        in_specs=[SMEM] * 2 + [VMEM] * 13,
        out_specs=[VMEM] * 3,
        scratch_shapes=[
            pltpu.VMEM((PLANES, TY + 2, ROWS, 128), bf16),
            pltpu.VMEM((2, GROWS, SPAN), bf16),
            pltpu.VMEM((128, SPAN), bf16),
        ],
        compiler_params=pltpu.CompilerParams(vmem_limit_bytes=40 * 1024 * 1024),
    )(
        coords, counts, feat, cot, mask, left, right, low, high,
        forward, backward, bias_wide, place_matrix(), window_matrix(), compact_matrix(),
    )

    n_gx = lax.axis_size("gx")
    rest = lax.axis_size("gy") * lax.axis_size("pair")
    chunk = RED // n_gx
    part = exchange(sums.reshape(n_gx, chunk, 128), "gx").sum(0)
    part = exchange(jnp.broadcast_to(part[None], (rest, chunk, 128)), ("gy", "pair")).sum(0)
    total = exchange(jnp.broadcast_to(part[None], (n_gx, chunk, 128)), "gx").reshape(RED, 128)
    total = total * (1.0 / math.sqrt(n_gx * rest * slots * 512))
    grad_weight = jnp.concatenate([total[0:KDIM, CH * d : CH * d + CH] for d in range(3)], axis=0)
    grad_bias = total[KDIM, CH : 2 * CH]
    full_shape = features.shape
    return out.reshape(full_shape), gin.reshape(full_shape), grad_weight, grad_bias


def solution(mesh):
    tiles = P("gx", "gy", "pair", None, None, None)
    in_specs = (
        tiles,
        tiles,
        P("gx", "gy", "pair", None, None),
        P("gx", "gy", "pair", None, None),
        P("gx", "gy", "pair"),
        P(),
        P(),
    )
    out_specs = (tiles, tiles, P(), P())
    return jax.shard_map(local, mesh=mesh, in_specs=in_specs, out_specs=out_specs, check_vma=False)
```

```python
import functools
import math

import jax
import jax.numpy as jnp
import numpy as np
from jax import lax
from jax.experimental import pallas as pl
from jax.experimental.pallas import tpu as pltpu
from jax.sharding import Mesh, PartitionSpec as P

TX = 4
TY = 4
CH = 32
ROWS = 2 * CH
PLANES = 8 * TX + 2
SPAN = 10 * 128
KDIM = 9 * CH
GROWS = KDIM + 16
RED = 256
PACK = 216
TAIL = KDIM - PACK
SLOTS = 8
HALF = SLOTS // 2


def face_matrix():
    m = np.zeros((512, 512), np.float32)
    for u in range(8):
        for c in range(8):
            m[64 * u + c, 16 * u + c] = 1
            m[64 * u + 56 + c, 128 + 16 * u + c] = 1
            m[8 * u + c, 256 + 16 * u + c] = 1
            m[448 + 8 * u + c, 384 + 16 * u + c] = 1
    return jnp.asarray(m, jnp.bfloat16)


def place_matrix():
    m = np.zeros((3, 128, 256), np.float32)
    for h in range(2):
        for b in range(8):
            for c in range(8):
                for tz in range(2):
                    m[tz, 64 * h + 8 * b + c, 128 * h + 16 * b + 8 * tz + c] = 1
                m[2, 64 * h + 8 * b + c, 128 * h + 10 * b + c] = 1
    return jnp.asarray(m, jnp.bfloat16)


def window_matrix():
    m = np.zeros((2, 256, 128), np.float32)
    for tz in range(2):
        for y in range(10):
            for z in range(10):
                gz = 8 * tz - 1 + z
                if gz < 0 or gz > 15:
                    continue
                if y == 0:
                    source = 128 + 112 + gz
                elif y == 9:
                    source = 128 + gz
                else:
                    source = 16 * (y - 1) + gz
                m[tz, source, 10 * y + z] = 1
    return jnp.asarray(m, jnp.bfloat16)


def compact_matrix():
    m = np.zeros((256, 128), np.float32)
    for h in range(2):
        for b in range(8):
            for c in range(8):
                m[128 * h + 10 * b + c, 64 * h + 8 * b + c] = 1
    return jnp.asarray(m, jnp.bfloat16)


def dot(a, b):
    return lax.dot_general(a, b, (((1,), (0,)), ((), ())), preferred_element_type=jnp.float32)


def live_row(mask_ref, counts, slot):
    on = jnp.where(slot < counts[0], 1, 0)
    return (mask_ref[pl.ds(slot, 1), :] * on).astype(jnp.float32)


def position(coords, slot):
    return coords[0, 0, slot], coords[1, 0, slot], coords[2, 0, slot]


def masked_tiles(counts, feat_ref, cot_ref, mask_ref, slot):
    live = live_row(mask_ref, counts, slot).astype(jnp.bfloat16)
    return jnp.concatenate([feat_ref[slot] * live, cot_ref[slot] * live], axis=0)


def fetch(sems, *pairs):
    copies = [pltpu.make_async_copy(source, target, sems.at[i]) for i, (source, target) in enumerate(pairs)]
    for copy in copies:
        copy.start()
    return copies


def finish_all(copies):
    for copy in copies:
        copy.wait()


def faces_kernel(
    coords_hbm, counts, feat_hbm, cot_hbm, mask_hbm, sel_hbm, xa_ref, xb_ref, ylo_ref, yhi_ref,
    coords, feat_ref, cot_ref, mask_ref, sel_ref, xlo_ref, xhi_ref, sems,
):
    copies = fetch(
        sems, (coords_hbm, coords), (feat_hbm, feat_ref), (cot_hbm, cot_ref), (mask_hbm, mask_ref), (sel_hbm, sel_ref)
    )
    for ref in (xlo_ref, xhi_ref, ylo_ref, yhi_ref):
        ref[...] = jnp.zeros_like(ref)
    finish_all(copies)
    tiles = [masked_tiles(counts, feat_ref, cot_ref, mask_ref, slot) for slot in range(SLOTS)]
    found = dot(jnp.concatenate(tiles, axis=0), sel_ref[...])
    for slot in range(SLOTS):
        tx, ty, tz = position(coords, slot)
        sides = ((ylo_ref, tx, ty == 0), (yhi_ref, tx, ty == TY - 1), (xlo_ref, ty, tx == 0), (xhi_ref, ty, tx == TX - 1))
        for block, (ref, place, on) in enumerate(sides):
            part = pltpu.roll(found[ROWS * slot : ROWS * slot + ROWS, 128 * block : 128 * block + 128], 8 * tz, 1)
            part = part * jnp.where(on, 1.0, 0.0)
            ref[place] = ref[place] + part.astype(jnp.bfloat16)
    deal(counts[1], xlo_ref, xhi_ref, xa_ref, xb_ref)


def deal(odd, low, high, first, second):
    @pl.when(odd == 0)
    def _():
        first[...] = high[...]
        second[...] = low[...]

    @pl.when(odd == 1)
    def _():
        first[...] = low[...]
        second[...] = high[...]


def undeal(odd, first, second, low, high):
    @pl.when(odd == 0)
    def _():
        low[...] = second[...]
        high[...] = first[...]

    @pl.when(odd == 1)
    def _():
        low[...] = first[...]
        high[...] = second[...]


def edges_kernel(counts, xa_ref, xb_ref, ylo_ref, yhi_ref, left_ref, right_ref, ya_ref, yb_ref, lo_ref, hi_ref):
    lane = lax.broadcasted_iota(jnp.int32, (ROWS, 128), 1)
    undeal(counts[1], xa_ref, xb_ref, left_ref, right_ref)
    lo_ref[0:TX] = ylo_ref[...]
    hi_ref[0:TX] = yhi_ref[...]

    def roll(value, shift):
        return pltpu.roll(value.astype(jnp.float32), shift, 1)

    lo = jnp.where(lane < 16, left_ref[0].astype(jnp.float32), roll(right_ref[0], 16))
    hi = jnp.where(lane < 16, roll(left_ref[TY - 1], 16), roll(right_ref[TY - 1], 32))
    lo_ref[TX] = lo.astype(jnp.bfloat16)
    hi_ref[TX] = hi.astype(jnp.bfloat16)
    deal(counts[2], lo_ref, hi_ref, ya_ref, yb_ref)


def turned_weights(weight):
    square = jnp.concatenate([weight, jnp.zeros((CH, 32), jnp.float32)], axis=1).T
    rows = []
    for dx in range(3):
        blocks = [square[CH * (26 - 9 * dx - k) : CH * (27 - 9 * dx - k)] for k in range(9)]
        rows.append(jnp.concatenate(blocks, axis=1))
    return jnp.concatenate(rows, axis=0)


def spread_kernel(
    coords_hbm, counts, feat_hbm, cot_hbm, mask_hbm, place_hbm, weight_hbm, u_ref, centre_ref, g_hbm, live_hbm, wf_hbm, wb_hbm,
    coords, feat_ref, cot_ref, mask_ref, place_ref, weight_ref, g_ref, live_ref, wf_ref, wb_ref, sems,
):
    copies = fetch(
        sems, (coords_hbm, coords), (feat_hbm, feat_ref), (cot_hbm, cot_ref), (mask_hbm, mask_ref), (place_hbm, place_ref),
        (weight_hbm, weight_ref),
    )
    u_ref[...] = jnp.zeros_like(u_ref)
    g_ref[...] = jnp.zeros_like(g_ref)
    finish_all(copies)
    for slot in range(SLOTS):
        tx, ty, tz = position(coords, slot)
        live_ref[slot : slot + 1, :] = live_row(mask_ref, counts, slot)
        tile = masked_tiles(counts, feat_ref, cot_ref, mask_ref, slot)
        stacked = jnp.concatenate([tile[:, 128 * j : 128 * j + 128] for j in range(4)], axis=0)
        spread = dot(stacked, place_ref[tz]).astype(jnp.bfloat16)
        middle = dot(stacked, place_ref[2]).astype(jnp.bfloat16)
        for a in range(8):
            row, col = ROWS * (a // 2), 128 * (a % 2)
            u_ref[8 * tx + a, ty] = u_ref[8 * tx + a, ty] + spread[row : row + CH, col : col + 128]
            g_ref[8 * tx + a, ty] = g_ref[8 * tx + a, ty] + spread[row + CH : row + ROWS, col : col + 128]
            centre_ref[slot, a] = middle[row + CH : row + ROWS, col : col + 128]
    weight = weight_ref[...]
    wf_ref[...] = jnp.concatenate([weight[:, KDIM * dx : KDIM * dx + KDIM] for dx in range(3)], axis=0)
    wb_ref[...] = turned_weights(weight.astype(jnp.float32)).astype(jnp.bfloat16)
    finish_all(fetch(sems, (g_ref, g_hbm), (live_ref, live_hbm), (wf_ref, wf_hbm), (wb_ref, wb_hbm)))


def join(field, counts, dense, left_ref, right_ref, ya_ref, yb_ref):
    odd = counts[2] == 1
    rows = slice(CH * field, CH * field + CH)
    for ty in range(TY):
        dense[0, ty + 1] = left_ref[ty, rows]
        dense[PLANES - 1, ty + 1] = right_ref[ty, rows]
    for group in range(TX + 1):
        first = ya_ref[group, rows].astype(jnp.float32)
        second = yb_ref[group, rows].astype(jnp.float32)
        lo = jnp.where(odd, first, second)
        hi = jnp.where(odd, second, first)
        for j in range(8 if group < TX else 2):
            plane = 1 + 8 * group + j if group < TX else j * (PLANES - 1)
            dense[plane, 0] = pltpu.roll(lo, (112 - 16 * j) % 128, 1).astype(jnp.bfloat16)
            dense[plane, TY + 1] = pltpu.roll(hi, (128 - 16 * j) % 128, 1).astype(jnp.bfloat16)


def window(coords, slot, dense, window_ref):
    tx, ty, tz = position(coords, slot)
    lane = lax.broadcasted_iota(jnp.int32, (10, CH, 128), 2)
    own = dense[pl.ds(8 * tx, 10), 1 + ty]
    below = dense[pl.ds(8 * tx, 10), ty]
    above = dense[pl.ds(8 * tx, 10), 2 + ty]
    rim = jnp.where(lane >= 112, below, jnp.where(lane < 16, above, jnp.zeros_like(own)))
    both = jnp.concatenate([own.reshape(10 * CH, 128), rim.reshape(10 * CH, 128)], axis=1)
    return dot(both, window_ref[tz])


def fill_columns(windows, columns, part):
    for k in range(9):
        shift = (k // 3) * 10 + k % 3
        moved = windows if shift == 0 else pltpu.roll(windows, 128 - shift, 1)
        moved = moved.astype(jnp.bfloat16)
        for p in range(10):
            columns[part, CH * k : CH * k + CH, 128 * p : 128 * p + 128] = moved[CH * p : CH * p + CH]


def gradient_kernel(
    coords_hbm, counts, u_ref, centre_ref, left_ref, right_ref, ya_ref, yb_ref, window_hbm,
    sums_ref, cut,
    coords, window_ref, dense, columns, centre, total, sems,
):
    copies = fetch(sems, (coords_hbm, coords), (window_hbm, window_ref))
    total[...] = jnp.zeros_like(total)
    centre[...] = jnp.zeros_like(centre)
    for part in range(2):
        columns[part, KDIM:GROWS, :] = jnp.ones((GROWS - KDIM, SPAN), jnp.bfloat16)
    for ty in range(TY):
        dense[1 : PLANES - 1, ty + 1] = u_ref[:, ty]
    join(0, counts, dense, left_ref, right_ref, ya_ref, yb_ref)
    finish_all(copies)
    steps = (counts[0] + 1) // 2

    def work(step, carry):
        for part in range(2):
            slot = 2 * step + part
            windows = window(coords, slot, dense, window_ref)
            cut[slot] = windows.astype(jnp.bfloat16)
            fill_columns(windows, columns, part)
            for a in range(8):
                plane = centre_ref[slot, a]
                for dx in range(3):
                    centre[part, CH * dx : CH * dx + CH, 128 * (a + dx) : 128 * (a + dx + 1)] = plane
        products = [
            lax.dot_general(columns[part], centre[part], (((1,), (1,)), ((), ())), preferred_element_type=jnp.float32)
            for part in range(2)
        ]
        total[...] += products[0] + products[1]
        return carry

    lax.fori_loop(0, steps, work, 0)
    sums_ref[...] = jnp.zeros_like(sums_ref)
    sums_ref[0:PACK, :] = total[0:PACK, :]
    sums_ref[PACK : PACK + 8, :] = total[KDIM : KDIM + 8, :]
    tail = total[PACK:KDIM, :]
    for dx in range(3):
        sums_ref[TAIL * dx : TAIL * dx + TAIL, 96:128] = pltpu.roll(tail, 96 - CH * dx, 1)[:, 96:128]


def cut_kernel(
    coords_hbm, counts, g_hbm, left_ref, right_ref, ya_ref, yb_ref, window_hbm, cut,
    coords, window_ref, dense, sems,
):
    inside = dense.at[pl.ds(1, PLANES - 2), pl.ds(1, TY)]
    copies = fetch(sems, (coords_hbm, coords), (window_hbm, window_ref), (g_hbm, inside))
    join(1, counts, dense, left_ref, right_ref, ya_ref, yb_ref)
    finish_all(copies)

    def work(step, carry):
        for part in range(2):
            cut[2 * step + part] = window(coords, 2 * step + part, dense, window_ref).astype(jnp.bfloat16)
        return carry

    lax.fori_loop(0, (counts[0] + 1) // 2, work, 0)


def conv_kernel(first, field, counts, cut, live, w_ref, bias_ref, compact_ref, *rest):
    out_ref, columns = rest[-2:]
    out_ref[...] = jnp.zeros_like(out_ref)

    def work(step, carry):
        for part in range(2):
            slot = 2 * step + part
            fill_columns(cut[first + slot].astype(jnp.float32), columns, part)
            z = dot(w_ref[...], columns[part])
            y = z[0:CH, 0:1024] + z[CH : 2 * CH, 128:1152] + z[2 * CH : 3 * CH, 256:1280]
            if field == 0:
                y = y + bias_ref[:, 0:1]
            y = y.astype(jnp.bfloat16)
            packed = dot(jnp.concatenate([y[:, 256 * j : 256 * j + 256] for j in range(4)], axis=0), compact_ref[...])
            rows = jnp.concatenate([packed[CH * j : CH * j + CH] for j in range(4)], axis=1)
            out_ref[slot] = (rows * live[pl.ds(first + slot, 1), :]).astype(jnp.bfloat16)
        return carry

    steps = (jnp.clip(counts[0] - first, 0, HALF) + 1) // 2
    lax.fori_loop(0, steps, work, 0)


def finish_kernel(scale, sums_ref, weight_ref, bias_ref):
    total = sums_ref[...] * scale
    turned = total.T
    pieces = []
    for dx in range(3):
        pieces.append(turned[CH * dx : CH * dx + CH, 0:PACK])
        pieces.append(turned[96:128, TAIL * dx : TAIL * dx + TAIL])
    weight_ref[...] = jnp.concatenate(pieces, axis=1)
    bias_ref[...] = pltpu.roll(total[PACK : PACK + 8], 128 - CH, 1)[0:1, 0:CH]


def swapped(axis, first):
    count = lax.axis_size(axis)
    pairs = [(i, i + 1) for i in range(first, count - 1, 2)]
    return pairs + [(j, i) for i, j in pairs]


def exchange(block, axes):
    return lax.all_to_all(block, axes, 0, 0, tiled=True)


GX = ("x", "core")
GY = ("zl", "y")
NEAR = ("x", "core", "zl")
FAR = ("y", "zh")
SMEM = pl.BlockSpec(memory_space=pltpu.SMEM)
VMEM = pl.BlockSpec(memory_space=pltpu.VMEM)
HBM = pl.BlockSpec(memory_space=pltpu.HBM)


def local(features, cotangent, masks, coords, counts, weight, bias):
    bf16, f32 = jnp.bfloat16, jnp.float32
    slots = features.shape[3]
    feat = features.reshape(slots, CH, 512)
    cot = cotangent.reshape(slots, CH, 512)
    mask = masks.reshape(slots, 512)
    coords = coords.reshape(3, 1, slots)
    odd = [lax.axis_index(axis) % 2 for axis in ("core", "y")]
    counts = jnp.stack([counts.reshape(()), *odd]).astype(jnp.int32)
    bias_wide = jnp.broadcast_to(bias[:, None], (CH, 128))
    params = pltpu.CompilerParams(vmem_limit_bytes=24 * 1024 * 1024)

    def shape(*dims, kind=bf16):
        return jax.ShapeDtypeStruct(dims, kind)

    def room(*dims, kind=bf16):
        return pltpu.VMEM(dims, kind)

    def sems(count):
        return pltpu.SemaphoreType.DMA((count,))

    def cost(flops, moved):
        return pl.CostEstimate(flops=flops, bytes_accessed=moved, transcendentals=0)

    spot = pltpu.SMEM((3, 1, slots), jnp.int32)
    args = [room(slots, CH, 512), room(slots, CH, 512), room(slots, 512, kind=jnp.int32)]
    held = [pltpu.with_memory_space_constraint(x, pltpu.HBM) for x in (coords, feat, cot, mask, face_matrix())]
    xa, xb, ylo, yhi = pl.pallas_call(
        faces_kernel,
        out_shape=[shape(4, ROWS, 128)] * 4,
        in_specs=[HBM, SMEM, HBM, HBM, HBM, HBM],
        out_specs=[VMEM] * 4,
        scratch_shapes=[spot, *args, room(512, 512), room(4, ROWS, 128), room(4, ROWS, 128), sems(5)],
        compiler_params=params,
    )(held[0], counts, *held[1:])
    left, right, ya, yb = pl.pallas_call(
        edges_kernel,
        out_shape=[shape(4, ROWS, 128)] * 2 + [shape(5, ROWS, 128)] * 2,
        in_specs=[SMEM] + [VMEM] * 4,
        out_specs=[VMEM] * 4,
        scratch_shapes=[room(5, ROWS, 128), room(5, ROWS, 128)],
        compiler_params=params,
    )(counts, lax.ppermute(xa, GX, swapped(GX, 0)), lax.ppermute(xb, GX, swapped(GX, 1)), ylo, yhi)
    mask_later, ya, yb = lax.optimization_barrier((mask, ya, yb))
    ya = lax.ppermute(ya, GY, swapped(GY, 0))
    yb = lax.ppermute(yb, GY, swapped(GY, 1))

    inner = shape(PLANES - 2, TY, CH, 128)
    u_inner, middles, g_inner, live, forward, backward = pl.pallas_call(
        spread_kernel,
        out_shape=[
            inner, shape(slots, 8, CH, 128), inner, shape(slots, 512, kind=f32), shape(3 * CH, KDIM), shape(3 * CH, KDIM)
        ],
        in_specs=[HBM, SMEM, HBM, HBM, HBM, HBM, HBM],
        out_specs=[VMEM] * 2 + [HBM] * 4,
        scratch_shapes=[
            spot, *args, room(3, 128, 256), room(CH, 3 * KDIM), room(PLANES - 2, TY, CH, 128), room(slots, 512, kind=f32),
            room(3 * CH, KDIM), room(3 * CH, KDIM), sems(6),
        ],
        compiler_params=params,
        cost_estimate=cost(1_000_000_000, 1_000_000),
    )(coords, counts, feat, cot, mask_later, place_matrix(), weight.T)

    cuts = shape(slots, 10 * CH, 128)
    windows = window_matrix()
    sums, u_cut = pl.pallas_call(
        gradient_kernel,
        out_shape=[shape(RED, 128, kind=f32), cuts],
        in_specs=[HBM, SMEM] + [VMEM] * 6 + [HBM],
        out_specs=[VMEM] * 2,
        scratch_shapes=[
            spot, room(2, 256, 128), room(PLANES, TY + 2, CH, 128), room(2, GROWS, SPAN),
            room(2, 128, SPAN), room(GROWS, 128, kind=f32), sems(2),
        ],
        compiler_params=params,
    )(coords, counts, u_inner, middles, left, right, ya, yb, windows)

    def convolve(field, half, cut, weights, begun):
        more = [] if begun is None else [begun]
        return pl.pallas_call(
            functools.partial(conv_kernel, HALF * half, field),
            grid=(1,),
            out_shape=shape(slots, CH, 512),
            in_specs=[SMEM] + [VMEM] * 5 + [HBM] * len(more),
            out_specs=pl.BlockSpec((HALF, CH, 512), lambda i: (half, 0, 0)),
            scratch_shapes=[room(2, KDIM, SPAN)],
            input_output_aliases={} if begun is None else {6: 0},
            compiler_params=params,
            cost_estimate=cost(3_000_000_000, 500_000),
        )(counts, cut, live, weights, bias_wide, compact_matrix(), *more)

    n_near, n_far = lax.axis_size(NEAR), lax.axis_size(FAR)
    chunk = RED // n_near
    part = exchange(sums.reshape(n_near, chunk, 128), NEAR)
    g_cut = pl.pallas_call(
        cut_kernel,
        out_shape=cuts,
        in_specs=[HBM, SMEM, HBM] + [VMEM] * 4 + [HBM],
        out_specs=VMEM,
        scratch_shapes=[spot, room(2, 256, 128), room(PLANES, TY + 2, CH, 128), sems(3)],
        compiler_params=params,
        cost_estimate=cost(1_000_000_000, 500_000),
    )(coords, counts, g_inner, left, right, ya, yb, windows)
    out = convolve(0, 0, u_cut, forward, None)
    part, out, g_cut = lax.optimization_barrier((part, out, g_cut))
    part = exchange(jnp.broadcast_to(part.sum(0)[None], (n_far, chunk, 128)), FAR)
    out = convolve(0, 1, u_cut, forward, out)
    gin = convolve(1, 0, g_cut, backward, None)
    part, out, gin = lax.optimization_barrier((part, out, gin))
    total = exchange(jnp.broadcast_to(part.sum(0)[None], (n_near, chunk, 128)), NEAR).reshape(RED, 128)
    gin = convolve(1, 1, g_cut, backward, gin)
    total, gin = lax.optimization_barrier((total, gin))
    scale = 1.0 / math.sqrt(n_near * n_far * slots * 512)
    grad_weight, grad_bias = pl.pallas_call(
        functools.partial(finish_kernel, scale),
        out_shape=[shape(CH, 3 * KDIM, kind=f32), shape(1, CH, kind=f32)],
        in_specs=[VMEM],
        out_specs=[VMEM] * 2,
        compiler_params=params,
    )(total)
    full_shape = features.shape
    return out.reshape(full_shape), gin.reshape(full_shape), grad_weight.T, grad_bias.reshape(CH)


def solution(mesh):
    fine = Mesh(mesh.devices.reshape(4, 2, 2, 4, 4), ("x", "core", "zl", "y", "zh"))
    spread = (GX, GY, "zh")
    tiles = P(*spread, None, None, None)
    in_specs = (tiles, tiles, P(*spread, None, None), P(*spread, None, None), P(*spread), P(), P())
    out_specs = (tiles, tiles, P(), P())
    return jax.shard_map(local, mesh=fine, in_specs=in_specs, out_specs=out_specs, check_vma=False)
```

```python
import functools
import math

import jax
import jax.numpy as jnp
import numpy as np
from jax import lax
from jax.experimental import pallas as pl
from jax.experimental.pallas import tpu as pltpu
from jax.sharding import Mesh, PartitionSpec as P

TX = 4
TY = 4
CH = 32
ROWS = 2 * CH
PLANES = 8 * TX + 2
SPAN = 10 * 128
KDIM = 9 * CH
GROWS = KDIM + 16
RED = 256
PACK = 216
TAIL = KDIM - PACK
SLOTS = 8
BATCH = 4


def face_matrix():
    m = np.zeros((512, 512), np.float32)
    for u in range(8):
        for c in range(8):
            m[64 * u + c, 16 * u + c] = 1
            m[64 * u + 56 + c, 128 + 16 * u + c] = 1
            m[8 * u + c, 256 + 16 * u + c] = 1
            m[448 + 8 * u + c, 384 + 16 * u + c] = 1
    return jnp.asarray(m, jnp.bfloat16)


def place_matrix():
    m = np.zeros((3, 128, 256), np.float32)
    for h in range(2):
        for b in range(8):
            for c in range(8):
                for tz in range(2):
                    m[tz, 64 * h + 8 * b + c, 128 * h + 16 * b + 8 * tz + c] = 1
                m[2, 64 * h + 8 * b + c, 128 * h + 10 * b + c] = 1
    return jnp.asarray(m, jnp.bfloat16)


def window_matrix():
    m = np.zeros((2, 256, 128), np.float32)
    for tz in range(2):
        for y in range(10):
            for z in range(10):
                gz = 8 * tz - 1 + z
                if gz < 0 or gz > 15:
                    continue
                if y == 0:
                    source = 128 + 112 + gz
                elif y == 9:
                    source = 128 + gz
                else:
                    source = 16 * (y - 1) + gz
                m[tz, source, 10 * y + z] = 1
    return jnp.asarray(m, jnp.bfloat16)


def compact_matrix():
    m = np.zeros((256, 128), np.float32)
    for h in range(2):
        for b in range(8):
            for c in range(8):
                m[128 * h + 10 * b + c, 64 * h + 8 * b + c] = 1
    return jnp.asarray(m, jnp.bfloat16)


def dot(a, b):
    return lax.dot_general(a, b, (((1,), (0,)), ((), ())), preferred_element_type=jnp.float32)


def live_row(mask_ref, facts_ref, slot):
    on = jnp.where(facts_ref[2:3, 0:1] > slot, 1.0, 0.0)
    return mask_ref[slot : slot + 1, :].astype(jnp.float32) * on


def position(coords, slot):
    return coords[0, 0, slot], coords[1, 0, slot], coords[2, 0, slot]


def masked_tiles(facts_ref, feat_ref, cot_ref, mask_ref, slot):
    live = live_row(mask_ref, facts_ref, slot).astype(jnp.bfloat16)
    return jnp.concatenate([feat_ref[slot] * live, cot_ref[slot] * live], axis=0)


def fetch(sems, *pairs):
    copies = [pltpu.make_async_copy(source, target, sems.at[i]) for i, (source, target) in enumerate(pairs)]
    for copy in copies:
        copy.start()
    return copies


def finish_all(copies):
    for copy in copies:
        copy.wait()


def pick(odd, one, other):
    odd = odd.astype(jnp.bfloat16)
    return one * odd + other * (1 - odd)


def faces_kernel(
    facts_ref, coords_hbm, feat_hbm, cot_hbm, mask_hbm, sel_hbm, xa_ref, xb_ref, ylo_ref, yhi_ref,
    coords, feat_ref, cot_ref, mask_ref, sel_ref, xlo_ref, xhi_ref, sems,
):
    copies = fetch(
        sems, (coords_hbm, coords), (feat_hbm, feat_ref), (cot_hbm, cot_ref), (mask_hbm, mask_ref), (sel_hbm, sel_ref)
    )
    for ref in (xlo_ref, xhi_ref, ylo_ref, yhi_ref):
        ref[...] = jnp.zeros_like(ref)
    finish_all(copies)
    tiles = [masked_tiles(facts_ref, feat_ref, cot_ref, mask_ref, slot) for slot in range(SLOTS)]
    found = dot(jnp.concatenate(tiles, axis=0), sel_ref[...])
    for slot in range(SLOTS):
        tx, ty, tz = position(coords, slot)
        sides = ((ylo_ref, tx, ty == 0), (yhi_ref, tx, ty == TY - 1), (xlo_ref, ty, tx == 0), (xhi_ref, ty, tx == TX - 1))
        for block, (ref, place, on) in enumerate(sides):
            part = pltpu.roll(found[ROWS * slot : ROWS * slot + ROWS, 128 * block : 128 * block + 128], 8 * tz, 1)
            part = part * jnp.where(on, 1.0, 0.0)
            ref[place] = ref[place] + part.astype(jnp.bfloat16)
    odd = facts_ref[0:1]
    xa_ref[...] = pick(odd, xlo_ref[...], xhi_ref[...])
    xb_ref[...] = pick(odd, xhi_ref[...], xlo_ref[...])


def edges_kernel(facts_ref, xa_ref, xb_ref, ylo_ref, yhi_ref, left_ref, right_ref, ya_ref, yb_ref):
    odd = facts_ref[0:1]
    left_ref[...] = pick(odd, xa_ref[...], xb_ref[...])
    right_ref[...] = pick(odd, xb_ref[...], xa_ref[...])
    lane = lax.broadcasted_iota(jnp.int32, (ROWS, 128), 1)

    def roll(value, shift):
        return pltpu.roll(value.astype(jnp.float32), shift, 1)

    lo = jnp.where(lane < 16, left_ref[0].astype(jnp.float32), roll(right_ref[0], 16)).astype(jnp.bfloat16)
    hi = jnp.where(lane < 16, roll(left_ref[TY - 1], 16), roll(right_ref[TY - 1], 32)).astype(jnp.bfloat16)
    odd = facts_ref[1:2]
    ya_ref[0:TX] = pick(odd, ylo_ref[...], yhi_ref[...])
    yb_ref[0:TX] = pick(odd, yhi_ref[...], ylo_ref[...])
    ya_ref[TX] = pick(odd, lo, hi)
    yb_ref[TX] = pick(odd, hi, lo)


def turned_weights(weight):
    square = jnp.concatenate([weight, jnp.zeros((CH, 32), jnp.float32)], axis=1).T
    rows = []
    for dx in range(3):
        blocks = [square[CH * (26 - 9 * dx - k) : CH * (27 - 9 * dx - k)] for k in range(9)]
        rows.append(jnp.concatenate(blocks, axis=1))
    return jnp.concatenate(rows, axis=0)


def spread_kernel(
    facts_ref, coords_hbm, feat_ref, cot_ref, mask_ref, place_ref, weight_ref, bias_hbm,
    u_ref, centre_ref, g_ref, live_ref, wf_ref, wb_ref, column_ref,
    coords, bias_ref, sems,
):
    copies = fetch(sems, (coords_hbm, coords), (bias_hbm, bias_ref))
    u_ref[...] = jnp.zeros_like(u_ref)
    g_ref[...] = jnp.zeros_like(g_ref)
    weight = weight_ref[...]
    wf_ref[...] = jnp.concatenate([weight[:, KDIM * dx : KDIM * dx + KDIM] for dx in range(3)], axis=0)
    wb_ref[...] = turned_weights(weight.astype(jnp.float32)).astype(jnp.bfloat16)
    finish_all(copies)
    diagonal = lax.broadcasted_iota(jnp.int32, (CH, CH), 0) == lax.broadcasted_iota(jnp.int32, (CH, CH), 1)
    column = jnp.sum(jnp.where(diagonal, bias_ref[...], 0.0), axis=1, keepdims=True)
    column_ref[...] = jnp.broadcast_to(column, (CH, 128))
    for slot in range(SLOTS):
        tx, ty, tz = position(coords, slot)
        live_ref[slot : slot + 1, :] = live_row(mask_ref, facts_ref, slot)
        tile = masked_tiles(facts_ref, feat_ref, cot_ref, mask_ref, slot)
        stacked = jnp.concatenate([tile[:, 128 * j : 128 * j + 128] for j in range(4)], axis=0)
        spread = dot(stacked, place_ref[tz]).astype(jnp.bfloat16)
        middle = dot(stacked, place_ref[2]).astype(jnp.bfloat16)
        for a in range(8):
            row, col = ROWS * (a // 2), 128 * (a % 2)
            u_ref[8 * tx + a, ty] = u_ref[8 * tx + a, ty] + spread[row : row + CH, col : col + 128]
            g_ref[8 * tx + a, ty] = g_ref[8 * tx + a, ty] + spread[row + CH : row + ROWS, col : col + 128]
            centre_ref[slot, a] = middle[row + CH : row + ROWS, col : col + 128]


def join(field, facts_ref, inner_ref, dense, left_ref, right_ref, ya_ref, yb_ref):
    odd = facts_ref[1:2] > 0.5
    rows = slice(CH * field, CH * field + CH)
    for ty in range(TY):
        dense[1 : PLANES - 1, ty + 1] = inner_ref[:, ty]
        dense[0, ty + 1] = left_ref[ty, rows]
        dense[PLANES - 1, ty + 1] = right_ref[ty, rows]
    for group in range(TX + 1):
        first = ya_ref[group, rows].astype(jnp.float32)
        second = yb_ref[group, rows].astype(jnp.float32)
        lo = jnp.where(odd, first, second)
        hi = jnp.where(odd, second, first)
        for j in range(8 if group < TX else 2):
            plane = 1 + 8 * group + j if group < TX else j * (PLANES - 1)
            dense[plane, 0] = pltpu.roll(lo, (112 - 16 * j) % 128, 1).astype(jnp.bfloat16)
            dense[plane, TY + 1] = pltpu.roll(hi, (128 - 16 * j) % 128, 1).astype(jnp.bfloat16)


def window(coords, slot, dense, window_ref):
    tx, ty, tz = position(coords, slot)
    lane = lax.broadcasted_iota(jnp.int32, (10, CH, 128), 2)
    own = dense[pl.ds(8 * tx, 10), 1 + ty]
    below = dense[pl.ds(8 * tx, 10), ty]
    above = dense[pl.ds(8 * tx, 10), 2 + ty]
    rim = jnp.where(lane >= 112, below, jnp.where(lane < 16, above, jnp.zeros_like(own)))
    both = jnp.concatenate([own.reshape(10 * CH, 128), rim.reshape(10 * CH, 128)], axis=1)
    return dot(both, window_ref[tz])


def fill_columns(windows, columns, slot):
    for k in range(9):
        shift = (k // 3) * 10 + k % 3
        moved = windows if shift == 0 else pltpu.roll(windows, 128 - shift, 1)
        moved = moved.astype(jnp.bfloat16)
        for p in range(10):
            columns[slot, CH * k : CH * k + CH, 128 * p : 128 * p + 128] = moved[CH * p : CH * p + CH]


def gradient_kernel(
    facts_ref, coords_hbm, u_ref, centre_ref, left_ref, right_ref, ya_ref, yb_ref, window_hbm,
    sums_ref, cut,
    coords, window_ref, dense, columns, centre, total, sems,
):
    copies = fetch(sems, (coords_hbm, coords), (window_hbm, window_ref))
    centre[...] = jnp.zeros_like(centre)
    sums_ref[...] = jnp.zeros_like(sums_ref)
    for slot in range(SLOTS):
        columns[slot, KDIM:GROWS, :] = jnp.ones((GROWS - KDIM, SPAN), jnp.bfloat16)
    join(0, facts_ref, u_ref, dense, left_ref, right_ref, ya_ref, yb_ref)
    finish_all(copies)
    for slot in range(SLOTS):
        windows = window(coords, slot, dense, window_ref)
        cut[slot] = windows.astype(jnp.bfloat16)
        fill_columns(windows, columns, slot)
        for a in range(8):
            plane = centre_ref[slot, a]
            for dx in range(3):
                centre[slot, CH * dx : CH * dx + CH, 128 * (a + dx) : 128 * (a + dx + 1)] = plane
    products = [
        lax.dot_general(columns[slot], centre[slot], (((1,), (1,)), ((), ())), preferred_element_type=jnp.float32)
        for slot in range(SLOTS)
    ]
    total[...] = sum(products[1:], products[0])
    sums_ref[0:PACK, :] = total[0:PACK, :]
    sums_ref[PACK : PACK + 8, :] = total[KDIM : KDIM + 8, :]
    tail = total[PACK:KDIM, :]
    for dx in range(3):
        sums_ref[TAIL * dx : TAIL * dx + TAIL, 96:128] = pltpu.roll(tail, 96 - CH * dx, 1)[:, 96:128]


def convolve_tiles(window_of, column_ref, live, w_ref, compact_ref, out_hbm, columns, out_ref, sems):
    copies = []
    for slot in range(SLOTS):
        fill_columns(window_of(slot), columns, slot)
        z = dot(w_ref[...], columns[slot])
        y = z[0:CH, 0:1024] + z[CH : 2 * CH, 128:1152] + z[2 * CH : 3 * CH, 256:1280]
        if column_ref is not None:
            y = y + column_ref[:, 0:1]
        y = y.astype(jnp.bfloat16)
        packed = dot(jnp.concatenate([y[:, 256 * j : 256 * j + 256] for j in range(4)], axis=0), compact_ref[...])
        rows = jnp.concatenate([packed[CH * j : CH * j + CH] for j in range(4)], axis=1)
        out_ref[slot] = (rows * live[slot : slot + 1, :]).astype(jnp.bfloat16)
        if slot % BATCH == BATCH - 1:
            done = pl.ds(slot + 1 - BATCH, BATCH)
            copies.append(pltpu.make_async_copy(out_ref.at[done], out_hbm.at[done], sems.at[slot // BATCH]))
            copies[-1].start()
    finish_all(copies)


def forward_kernel(cut, column_ref, live, w_ref, compact_ref, out_hbm, columns, out_ref, sems):
    convolve_tiles(
        lambda slot: cut[slot].astype(jnp.float32), column_ref, live, w_ref, compact_ref, out_hbm, columns, out_ref, sems
    )


def backward_kernel(
    facts_ref, coords_hbm, g_ref, left_ref, right_ref, ya_ref, yb_ref, window_ref, live, w_ref, compact_ref, out_hbm,
    coords, dense, columns, out_ref, start_sems, sems,
):
    copies = fetch(start_sems, (coords_hbm, coords))
    join(1, facts_ref, g_ref, dense, left_ref, right_ref, ya_ref, yb_ref)
    finish_all(copies)
    convolve_tiles(
        lambda slot: window(coords, slot, dense, window_ref), None, live, w_ref, compact_ref, out_hbm, columns, out_ref, sems
    )


def share_kernel(parts_ref, out_ref):
    total = parts_ref[0]
    for i in range(1, parts_ref.shape[0]):
        total = total + parts_ref[i]
    for i in range(out_ref.shape[0]):
        out_ref[i] = total


def finish_kernel(scale, sums_ref, weight_ref, bias_ref):
    total = sums_ref[...] * scale
    turned = total.T
    pieces = []
    for dx in range(3):
        pieces.append(turned[CH * dx : CH * dx + CH, 0:PACK])
        pieces.append(turned[96:128, TAIL * dx : TAIL * dx + TAIL])
    weight_ref[...] = jnp.concatenate(pieces, axis=1)
    bias_ref[...] = pltpu.roll(total[PACK : PACK + 8], 128 - CH, 1)[0:1, 0:CH]


def swapped(axis, first):
    count = lax.axis_size(axis)
    pairs = [(i, i + 1) for i in range(first, count - 1, 2)]
    return pairs + [(j, i) for i, j in pairs]


def exchange(block, axes):
    return lax.all_to_all(block, axes, 0, 0, tiled=True)


GX = ("x", "core")
GY = ("zl", "y")
NEAR = ("x", "core", "zl")
FAR = ("y", "zh")
SMEM = pl.BlockSpec(memory_space=pltpu.SMEM)
VMEM = pl.BlockSpec(memory_space=pltpu.VMEM)
HBM = pl.BlockSpec(memory_space=pltpu.HBM)


def local(features, cotangent, masks, coords, counts, weight, bias):
    bf16, f32 = jnp.bfloat16, jnp.float32
    slots = features.shape[3]
    feat = features.reshape(slots, CH, 512)
    cot = cotangent.reshape(slots, CH, 512)
    mask = masks.reshape(slots, 512)
    odd = [lax.axis_index(axis) % 2 for axis in ("core", "y")]
    facts = jnp.stack([*odd, counts.reshape(())]).astype(f32)
    facts = jnp.broadcast_to(jnp.pad(facts, (0, 5))[:, None], (8, 128))
    params = pltpu.CompilerParams(vmem_limit_bytes=24 * 1024 * 1024)

    def shape(*dims, kind=bf16):
        return jax.ShapeDtypeStruct(dims, kind)

    def room(*dims, kind=bf16):
        return pltpu.VMEM(dims, kind)

    def sems(count):
        return pltpu.SemaphoreType.DMA((count,))

    def cost(flops, moved):
        return pl.CostEstimate(flops=flops, bytes_accessed=moved, transcendentals=0)

    def held(x):
        return pltpu.with_memory_space_constraint(x, pltpu.HBM)

    spot = pltpu.SMEM((3, 1, slots), jnp.int32)
    coords = held(coords.reshape(3, 1, slots))
    xa, xb, ylo, yhi = pl.pallas_call(
        faces_kernel,
        out_shape=[shape(4, ROWS, 128)] * 4,
        in_specs=[VMEM] + [HBM] * 5,
        out_specs=[VMEM] * 4,
        scratch_shapes=[
            spot, room(slots, CH, 512), room(slots, CH, 512), room(slots, 512, kind=jnp.int32), room(512, 512),
            room(4, ROWS, 128), room(4, ROWS, 128), sems(5),
        ],
        compiler_params=params,
    )(facts, coords, held(feat), held(cot), held(mask), held(face_matrix()))
    xb = lax.ppermute(xb, GX, swapped(GX, 1))
    xa = lax.ppermute(xa, GX, swapped(GX, 0))
    left, right, ya, yb = pl.pallas_call(
        edges_kernel,
        out_shape=[shape(4, ROWS, 128)] * 2 + [shape(5, ROWS, 128)] * 2,
        in_specs=[VMEM] * 5,
        out_specs=[VMEM] * 4,
        compiler_params=params,
    )(facts, xa, xb, ylo, yhi)
    facts_later, ya, yb = lax.optimization_barrier((facts, ya, yb))
    ya = lax.ppermute(ya, GY, swapped(GY, 0))
    yb = lax.ppermute(yb, GY, swapped(GY, 1))

    inner = shape(PLANES - 2, TY, CH, 128)
    u_inner, middles, g_inner, live, forward, backward, column = pl.pallas_call(
        spread_kernel,
        out_shape=[
            inner, shape(slots, 8, CH, 128), inner, shape(slots, 512, kind=f32), shape(3 * CH, KDIM), shape(3 * CH, KDIM),
            shape(CH, 128, kind=f32),
        ],
        in_specs=[VMEM, HBM] + [VMEM] * 5 + [HBM],
        out_specs=[VMEM] * 7,
        scratch_shapes=[spot, room(1, CH, kind=f32), sems(2)],
        compiler_params=params,
        cost_estimate=cost(1_000_000_000, 1_000_000),
    )(facts_later, coords, feat, cot, mask, place_matrix(), weight.T, held(bias.reshape(1, CH)))

    windows = window_matrix()
    sums, u_cut = pl.pallas_call(
        gradient_kernel,
        out_shape=[shape(RED, 128, kind=f32), shape(slots, 10 * CH, 128)],
        in_specs=[VMEM, HBM] + [VMEM] * 6 + [HBM],
        out_specs=[VMEM] * 2,
        scratch_shapes=[
            spot, room(2, 256, 128), room(PLANES, TY + 2, CH, 128), room(slots, GROWS, SPAN), room(slots, 128, SPAN),
            room(GROWS, 128, kind=f32), sems(2),
        ],
        compiler_params=params,
    )(facts, coords, u_inner, middles, left, right, ya, yb, windows)

    def share(parts, copies):
        return pl.pallas_call(
            share_kernel,
            out_shape=shape(copies, chunk, 128, kind=f32),
            in_specs=[VMEM],
            out_specs=VMEM,
            compiler_params=params,
        )(parts)

    n_near, n_far = lax.axis_size(NEAR), lax.axis_size(FAR)
    chunk = RED // n_near
    compact = compact_matrix()
    room_out = [room(slots, KDIM, SPAN), room(slots, CH, 512)]
    part = exchange(sums.reshape(n_near, chunk, 128), NEAR)
    out = pl.pallas_call(
        forward_kernel,
        out_shape=shape(slots, CH, 512),
        in_specs=[VMEM] * 5,
        out_specs=HBM,
        scratch_shapes=[*room_out, sems(slots // BATCH)],
        compiler_params=params,
        cost_estimate=cost(200_000_000, 100_000),
    )(u_cut, column, live, forward, compact)
    part, out = lax.optimization_barrier((part, out))
    part = exchange(share(part, n_far), FAR)
    gin = pl.pallas_call(
        backward_kernel,
        out_shape=shape(slots, CH, 512),
        in_specs=[VMEM, HBM] + [VMEM] * 9,
        out_specs=HBM,
        scratch_shapes=[spot, room(PLANES, TY + 2, CH, 128), *room_out, sems(1), sems(slots // BATCH)],
        compiler_params=params,
        cost_estimate=cost(200_000_000, 100_000),
    )(facts, coords, g_inner, left, right, ya, yb, windows, live, backward, compact)
    part, gin = lax.optimization_barrier((part, gin))
    total = exchange(share(part, n_near), NEAR).reshape(RED, 128)
    scale = 1.0 / math.sqrt(n_near * n_far * slots * 512)
    grad_weight, grad_bias = pl.pallas_call(
        functools.partial(finish_kernel, scale),
        out_shape=[shape(CH, 3 * KDIM, kind=f32), shape(1, CH, kind=f32)],
        in_specs=[VMEM],
        out_specs=[VMEM] * 2,
        compiler_params=params,
    )(total)
    full_shape = features.shape
    return out.reshape(full_shape), gin.reshape(full_shape), grad_weight.T, grad_bias.reshape(CH)


def solution(mesh):
    fine = Mesh(mesh.devices.reshape(4, 2, 2, 4, 4), ("x", "core", "zl", "y", "zh"))
    spread = (GX, GY, "zh")
    tiles = P(*spread, None, None, None)
    in_specs = (tiles, tiles, P(*spread, None, None), P(*spread, None, None), P(*spread), P(), P())
    out_specs = (tiles, tiles, P(), P())
    return jax.shard_map(local, mesh=fine, in_specs=in_specs, out_specs=out_specs, check_vma=False)
```

```python
import functools
import math

import jax
import jax.numpy as jnp
import numpy as np
from jax import lax
from jax.experimental import pallas as pl
from jax.experimental.pallas import tpu as pltpu
from jax.sharding import Mesh, PartitionSpec as P

TX = 4
TY = 4
CH = 32
ROWS = 2 * CH
PLANES = 8 * TX + 2
SPAN = 10 * 128
KDIM = 9 * CH
GROWS = KDIM + 16
RED = 256
PACK = 216
TAIL = KDIM - PACK
SLOTS = 8
BATCH = 4


def face_matrix():
    m = np.zeros((512, 512), np.float32)
    for u in range(8):
        for c in range(8):
            m[64 * u + c, 16 * u + c] = 1
            m[64 * u + 56 + c, 128 + 16 * u + c] = 1
            m[8 * u + c, 256 + 16 * u + c] = 1
            m[448 + 8 * u + c, 384 + 16 * u + c] = 1
    return jnp.asarray(m, jnp.bfloat16)


def place_matrix():
    m = np.zeros((3, 128, 256), np.float32)
    for h in range(2):
        for b in range(8):
            for c in range(8):
                for tz in range(2):
                    m[tz, 64 * h + 8 * b + c, 128 * h + 16 * b + 8 * tz + c] = 1
                m[2, 64 * h + 8 * b + c, 128 * h + 10 * b + c] = 1
    return jnp.asarray(m, jnp.bfloat16)


def window_matrix():
    m = np.zeros((2, 256, 128), np.float32)
    for tz in range(2):
        for y in range(10):
            for z in range(10):
                gz = 8 * tz - 1 + z
                if gz < 0 or gz > 15:
                    continue
                if y == 0:
                    source = 128 + 112 + gz
                elif y == 9:
                    source = 128 + gz
                else:
                    source = 16 * (y - 1) + gz
                m[tz, source, 10 * y + z] = 1
    return jnp.asarray(m, jnp.bfloat16)


def compact_matrix():
    m = np.zeros((256, 128), np.float32)
    for h in range(2):
        for b in range(8):
            for c in range(8):
                m[128 * h + 10 * b + c, 64 * h + 8 * b + c] = 1
    return jnp.asarray(m, jnp.bfloat16)


def dot(a, b):
    return lax.dot_general(a, b, (((1,), (0,)), ((), ())), preferred_element_type=jnp.float32)


def live_row(mask_ref, facts_ref, slot):
    on = jnp.where(facts_ref[2:3, 0:1] > slot, 1.0, 0.0)
    return mask_ref[slot : slot + 1, :].astype(jnp.float32) * on


def position(coords, slot):
    return coords[0, 0, slot], coords[1, 0, slot], coords[2, 0, slot]


def masked_tiles(facts_ref, feat_ref, cot_ref, mask_ref, slot):
    live = live_row(mask_ref, facts_ref, slot).astype(jnp.bfloat16)
    return jnp.concatenate([feat_ref[slot] * live, cot_ref[slot] * live], axis=0)


def fetch(sems, *pairs):
    copies = [pltpu.make_async_copy(source, target, sems.at[i]) for i, (source, target) in enumerate(pairs)]
    for copy in copies:
        copy.start()
    return copies


def finish_all(copies):
    for copy in copies:
        copy.wait()


def pick(odd, one, other):
    odd = odd.astype(jnp.bfloat16)
    return one * odd + other * (1 - odd)


def faces_kernel(
    facts_ref, coords_hbm, feat_hbm, cot_hbm, mask_hbm, sel_hbm, xa_ref, xb_ref, xlo_ref, ylo_ref, yhi_ref,
    coords, feat_ref, cot_ref, mask_ref, sel_ref, xhi_ref, sems,
):
    copies = fetch(
        sems, (coords_hbm, coords), (feat_hbm, feat_ref), (cot_hbm, cot_ref), (mask_hbm, mask_ref), (sel_hbm, sel_ref)
    )
    for ref in (xlo_ref, xhi_ref, ylo_ref, yhi_ref):
        ref[...] = jnp.zeros_like(ref)
    finish_all(copies)
    tiles = [masked_tiles(facts_ref, feat_ref, cot_ref, mask_ref, slot) for slot in range(SLOTS)]
    found = dot(jnp.concatenate(tiles, axis=0), sel_ref[...])
    for slot in range(SLOTS):
        tx, ty, tz = position(coords, slot)
        sides = ((ylo_ref, tx, ty == 0), (yhi_ref, tx, ty == TY - 1), (xlo_ref, ty, tx == 0), (xhi_ref, ty, tx == TX - 1))
        for block, (ref, place, on) in enumerate(sides):
            part = pltpu.roll(found[ROWS * slot : ROWS * slot + ROWS, 128 * block : 128 * block + 128], 8 * tz, 1)
            part = part * jnp.where(on, 1.0, 0.0)
            ref[place] = ref[place] + part.astype(jnp.bfloat16)
    odd = facts_ref[0:1]
    xa_ref[...] = pick(odd, xlo_ref[...], xhi_ref[...])
    xb_ref[...] = pick(odd, xhi_ref[...], xlo_ref[...])


def edges_kernel(facts_ref, xa_ref, xb_ref, ylo_ref, yhi_ref, left_ref, right_ref, ya_ref, yb_ref):
    odd = facts_ref[0:1]
    left_ref[...] = pick(odd, xa_ref[...], xb_ref[...])
    right_ref[...] = pick(odd, xb_ref[...], xa_ref[...])
    lane = lax.broadcasted_iota(jnp.int32, (ROWS, 128), 1)

    def roll(value, shift):
        return pltpu.roll(value.astype(jnp.float32), shift, 1)

    lo = jnp.where(lane < 16, left_ref[0].astype(jnp.float32), roll(right_ref[0], 16)).astype(jnp.bfloat16)
    hi = jnp.where(lane < 16, roll(left_ref[TY - 1], 16), roll(right_ref[TY - 1], 32)).astype(jnp.bfloat16)
    odd = facts_ref[1:2]
    ya_ref[0:TX] = pick(odd, ylo_ref[...], yhi_ref[...])
    yb_ref[0:TX] = pick(odd, yhi_ref[...], ylo_ref[...])
    ya_ref[TX] = pick(odd, lo, hi)
    yb_ref[TX] = pick(odd, hi, lo)


def turned_weights(weight):
    square = jnp.concatenate([weight, jnp.zeros((CH, 32), jnp.float32)], axis=1).T
    rows = []
    for dx in range(3):
        blocks = [square[CH * (26 - 9 * dx - k) : CH * (27 - 9 * dx - k)] for k in range(9)]
        rows.append(jnp.concatenate(blocks, axis=1))
    return jnp.concatenate(rows, axis=0)


def spread_kernel(
    facts_ref, coords_hbm, feat_ref, cot_ref, mask_ref, place_ref, weight_ref, bias_hbm,
    u_ref, centre_ref, g_ref, live_ref, wf_ref, wb_ref, column_ref,
    coords, bias_ref, sems,
):
    copies = fetch(sems, (coords_hbm, coords), (bias_hbm, bias_ref))
    u_ref[...] = jnp.zeros_like(u_ref)
    g_ref[...] = jnp.zeros_like(g_ref)
    weight = weight_ref[...]
    wf_ref[...] = jnp.concatenate([weight[:, KDIM * dx : KDIM * dx + KDIM] for dx in range(3)], axis=0)
    wb_ref[...] = turned_weights(weight.astype(jnp.float32)).astype(jnp.bfloat16)
    finish_all(copies)
    diagonal = lax.broadcasted_iota(jnp.int32, (CH, CH), 0) == lax.broadcasted_iota(jnp.int32, (CH, CH), 1)
    column = jnp.sum(jnp.where(diagonal, bias_ref[...], 0.0), axis=1, keepdims=True)
    column_ref[...] = jnp.broadcast_to(column, (CH, 128))
    for slot in range(SLOTS):
        tx, ty, tz = position(coords, slot)
        live_ref[slot : slot + 1, :] = live_row(mask_ref, facts_ref, slot)
        tile = masked_tiles(facts_ref, feat_ref, cot_ref, mask_ref, slot)
        stacked = jnp.concatenate([tile[:, 128 * j : 128 * j + 128] for j in range(4)], axis=0)
        spread = dot(stacked, place_ref[tz]).astype(jnp.bfloat16)
        middle = dot(stacked, place_ref[2]).astype(jnp.bfloat16)
        for a in range(8):
            row, col = ROWS * (a // 2), 128 * (a % 2)
            u_ref[8 * tx + a, ty] = u_ref[8 * tx + a, ty] + spread[row : row + CH, col : col + 128]
            g_ref[8 * tx + a, ty] = g_ref[8 * tx + a, ty] + spread[row + CH : row + ROWS, col : col + 128]
            centre_ref[slot, a] = middle[row + CH : row + ROWS, col : col + 128]


def join(field, facts_ref, inner_ref, dense, left_ref, right_ref, ya_ref, yb_ref):
    odd = facts_ref[1:2] > 0.5
    rows = slice(CH * field, CH * field + CH)
    for ty in range(TY):
        dense[1 : PLANES - 1, ty + 1] = inner_ref[:, ty]
        dense[0, ty + 1] = left_ref[ty, rows]
        dense[PLANES - 1, ty + 1] = right_ref[ty, rows]
    for group in range(TX + 1):
        first = ya_ref[group, rows].astype(jnp.float32)
        second = yb_ref[group, rows].astype(jnp.float32)
        lo = jnp.where(odd, first, second)
        hi = jnp.where(odd, second, first)
        for j in range(8 if group < TX else 2):
            plane = 1 + 8 * group + j if group < TX else j * (PLANES - 1)
            dense[plane, 0] = pltpu.roll(lo, (112 - 16 * j) % 128, 1).astype(jnp.bfloat16)
            dense[plane, TY + 1] = pltpu.roll(hi, (128 - 16 * j) % 128, 1).astype(jnp.bfloat16)


def window(coords, slot, dense, window_ref):
    tx, ty, tz = position(coords, slot)
    lane = lax.broadcasted_iota(jnp.int32, (10, CH, 128), 2)
    own = dense[pl.ds(8 * tx, 10), 1 + ty]
    below = dense[pl.ds(8 * tx, 10), ty]
    above = dense[pl.ds(8 * tx, 10), 2 + ty]
    rim = jnp.where(lane >= 112, below, jnp.where(lane < 16, above, jnp.zeros_like(own)))
    both = jnp.concatenate([own.reshape(10 * CH, 128), rim.reshape(10 * CH, 128)], axis=1)
    return dot(both, window_ref[tz])


def fill_columns(windows, columns, slot):
    for k in range(9):
        shift = (k // 3) * 10 + k % 3
        moved = windows if shift == 0 else pltpu.roll(windows, 128 - shift, 1)
        moved = moved.astype(jnp.bfloat16)
        for p in range(10):
            columns[slot, CH * k : CH * k + CH, 128 * p : 128 * p + 128] = moved[CH * p : CH * p + CH]


def gradient_kernel(
    coords_hbm, u_ref, centre_ref, window_hbm, total_ref, coords, window_ref, dense, columns, centre, sems
):
    copies = fetch(sems, (coords_hbm, coords), (window_hbm, window_ref))
    centre[...] = jnp.zeros_like(centre)
    for slot in range(SLOTS):
        columns[slot, KDIM:GROWS, :] = jnp.ones((GROWS - KDIM, SPAN), jnp.bfloat16)
    for plane in (0, PLANES - 1):
        dense[plane] = jnp.zeros((TY + 2, CH, 128), jnp.bfloat16)
    for ty in (0, TY + 1):
        dense[:, ty] = jnp.zeros((PLANES, CH, 128), jnp.bfloat16)
    for ty in range(TY):
        dense[1 : PLANES - 1, ty + 1] = u_ref[:, ty]
    finish_all(copies)
    for slot in range(SLOTS):
        fill_columns(window(coords, slot, dense, window_ref), columns, slot)
        for a in range(8):
            plane = centre_ref[slot, a]
            for dx in range(3):
                centre[slot, CH * dx : CH * dx + CH, 128 * (a + dx) : 128 * (a + dx + 1)] = plane
    products = [dot_nt(columns[slot], centre[slot]) for slot in range(SLOTS)]
    total_ref[...] = sum(products[1:], products[0])


def dot_nt(a, b):
    return lax.dot_general(a, b, (((1,), (1,)), ((), ())), preferred_element_type=jnp.float32)


def face_product(u, g):
    lane = lax.broadcasted_iota(jnp.int32, u.shape, 1)
    z = lane % 16
    width = u.shape[1]
    rows = [jnp.where(z == 0, 0.0, pltpu.roll(u, 1, 1)), u, jnp.where(z == 15, 0.0, pltpu.roll(u, width - 1, 1))]
    level = jnp.where(lane < 128, 0.0, g)
    columns = [pltpu.roll(g, width - 16, 1), level, pltpu.roll(g, 16, 1), jnp.zeros_like(g)]
    return dot_nt(
        jnp.concatenate(rows, axis=0).astype(jnp.bfloat16), jnp.concatenate(columns, axis=0).astype(jnp.bfloat16)
    )


def border_kernel(facts_ref, total_ref, left_ref, xlo_ref, ya_ref, yb_ref, ylo_ref, sums_ref, total):
    odd = facts_ref[1:2] > 0.5
    lane = lax.broadcasted_iota(jnp.int32, (ROWS, 128), 1)
    nothing = jnp.zeros((ROWS, 128), jnp.float32)

    def wide(first, parts):
        return jnp.concatenate([first] + [part.astype(jnp.float32) for part in parts], axis=1)

    def corner(tile):
        return jnp.where(lane >= 112, pltpu.roll(tile.astype(jnp.float32), 112, 1), 0.0)

    low = [jnp.where(odd, ya_ref[i].astype(jnp.float32), yb_ref[i].astype(jnp.float32)) for i in range(TX + 1)]
    x_far = wide(nothing, [left_ref[i] for i in range(TY)])
    x_own = wide(nothing, [xlo_ref[i] for i in range(TY)])
    y_far = wide(corner(low[TX]), low[0:TX])
    y_own = wide(corner(left_ref[0]), [ylo_ref[i] for i in range(TX)])
    third = 3 * CH
    total[...] = total_ref[...]
    total[0:third] += face_product(y_far[0:CH], y_own[CH:ROWS])
    total[2 * third : 3 * third] += face_product(y_own[0:CH], y_far[CH:ROWS])
    column = lax.broadcasted_iota(jnp.int32, (third, 128), 1)
    before = face_product(x_far[0:CH], x_own[CH:ROWS])
    after = face_product(x_own[0:CH], x_far[CH:ROWS])
    for dy in range(3):
        one = jnp.where(column < CH, pltpu.roll(before, (128 - CH * dy) % 128, 1), 0.0)
        two = jnp.where((column >= 2 * CH) & (column < third), pltpu.roll(after, (128 + 2 * CH - CH * dy) % 128, 1), 0.0)
        total[third * dy : third * dy + third] += one + two
    sums_ref[...] = jnp.zeros_like(sums_ref)
    sums_ref[0:PACK, :] = total[0:PACK, :]
    sums_ref[PACK : PACK + 8, :] = total[KDIM : KDIM + 8, :]
    tail = total[PACK:KDIM, :]
    for dx in range(3):
        sums_ref[TAIL * dx : TAIL * dx + TAIL, 96:128] = pltpu.roll(tail, 96 - CH * dx, 1)[:, 96:128]


def convolve_tiles(window_of, column_ref, live, w_ref, compact_ref, out_hbm, columns, out_ref, sems):
    copies = []
    for slot in range(SLOTS):
        fill_columns(window_of(slot), columns, slot)
        z = dot(w_ref[...], columns[slot])
        y = z[0:CH, 0:1024] + z[CH : 2 * CH, 128:1152] + z[2 * CH : 3 * CH, 256:1280]
        if column_ref is not None:
            y = y + column_ref[:, 0:1]
        y = y.astype(jnp.bfloat16)
        packed = dot(jnp.concatenate([y[:, 256 * j : 256 * j + 256] for j in range(4)], axis=0), compact_ref[...])
        rows = jnp.concatenate([packed[CH * j : CH * j + CH] for j in range(4)], axis=1)
        out_ref[slot] = (rows * live[slot : slot + 1, :]).astype(jnp.bfloat16)
        if slot % BATCH == BATCH - 1:
            done = pl.ds(slot + 1 - BATCH, BATCH)
            copies.append(pltpu.make_async_copy(out_ref.at[done], out_hbm.at[done], sems.at[slot // BATCH]))
            copies[-1].start()
    finish_all(copies)


def tiles_kernel(
    field, facts_ref, coords_hbm, inner_ref, left_ref, right_ref, ya_ref, yb_ref, window_ref, live, w_ref, compact_ref, column_ref,
    out_hbm, coords, dense, columns, out_ref, start_sems, sems,
):
    copies = fetch(start_sems, (coords_hbm, coords))
    join(field, facts_ref, inner_ref, dense, left_ref, right_ref, ya_ref, yb_ref)
    finish_all(copies)
    convolve_tiles(
        lambda slot: window(coords, slot, dense, window_ref), column_ref if field == 0 else None, live, w_ref, compact_ref,
        out_hbm, columns, out_ref, sems,
    )


def share_kernel(parts_ref, out_ref):
    total = parts_ref[0]
    for i in range(1, parts_ref.shape[0]):
        total = total + parts_ref[i]
    for i in range(out_ref.shape[0]):
        out_ref[i] = total


def finish_kernel(scale, sums_ref, weight_ref, bias_ref):
    total = sums_ref[...] * scale
    turned = total.T
    pieces = []
    for dx in range(3):
        pieces.append(turned[CH * dx : CH * dx + CH, 0:PACK])
        pieces.append(turned[96:128, TAIL * dx : TAIL * dx + TAIL])
    weight_ref[...] = jnp.concatenate(pieces, axis=1)
    bias_ref[...] = pltpu.roll(total[PACK : PACK + 8], 128 - CH, 1)[0:1, 0:CH]


def swapped(axis, first):
    count = lax.axis_size(axis)
    pairs = [(i, i + 1) for i in range(first, count - 1, 2)]
    return pairs + [(j, i) for i, j in pairs]


def exchange(block, axes):
    return lax.all_to_all(block, axes, 0, 0, tiled=True)


GX = ("x", "core")
GY = ("zl", "y")
NEAR = ("x", "core", "zl")
FAR = ("y", "zh")
SMEM = pl.BlockSpec(memory_space=pltpu.SMEM)
VMEM = pl.BlockSpec(memory_space=pltpu.VMEM)
HBM = pl.BlockSpec(memory_space=pltpu.HBM)


def local(features, cotangent, masks, coords, counts, weight, bias):
    bf16, f32 = jnp.bfloat16, jnp.float32
    slots = features.shape[3]
    feat = features.reshape(slots, CH, 512)
    cot = cotangent.reshape(slots, CH, 512)
    mask = masks.reshape(slots, 512)
    odd = [lax.axis_index(axis) % 2 for axis in ("core", "y")]
    facts = jnp.stack([*odd, counts.reshape(())]).astype(f32)
    facts = jnp.broadcast_to(jnp.pad(facts, (0, 5))[:, None], (8, 128))
    params = pltpu.CompilerParams(vmem_limit_bytes=24 * 1024 * 1024)

    def shape(*dims, kind=bf16):
        return jax.ShapeDtypeStruct(dims, kind)

    def room(*dims, kind=bf16):
        return pltpu.VMEM(dims, kind)

    def sems(count):
        return pltpu.SemaphoreType.DMA((count,))

    def cost(flops, moved):
        return pl.CostEstimate(flops=flops, bytes_accessed=moved, transcendentals=0)

    def held(x):
        return pltpu.with_memory_space_constraint(x, pltpu.HBM)

    spot = pltpu.SMEM((3, 1, slots), jnp.int32)
    coords = held(coords.reshape(3, 1, slots))
    xa, xb, xlo, ylo, yhi = pl.pallas_call(
        faces_kernel,
        out_shape=[shape(4, ROWS, 128)] * 5,
        in_specs=[VMEM] + [HBM] * 5,
        out_specs=[VMEM] * 5,
        scratch_shapes=[
            spot, room(slots, CH, 512), room(slots, CH, 512), room(slots, 512, kind=jnp.int32), room(512, 512),
            room(4, ROWS, 128), sems(5),
        ],
        compiler_params=params,
    )(facts, coords, held(feat), held(cot), held(mask), held(face_matrix()))
    xb = lax.ppermute(xb, GX, swapped(GX, 1))
    xa = lax.ppermute(xa, GX, swapped(GX, 0))
    inner = shape(PLANES - 2, TY, CH, 128)
    u_inner, middles, g_inner, live, forward, backward, column = pl.pallas_call(
        spread_kernel,
        out_shape=[
            inner, shape(slots, 8, CH, 128), inner, shape(slots, 512, kind=f32), shape(3 * CH, KDIM), shape(3 * CH, KDIM),
            shape(CH, 128, kind=f32),
        ],
        in_specs=[VMEM, HBM] + [VMEM] * 5 + [HBM],
        out_specs=[VMEM] * 7,
        scratch_shapes=[spot, room(1, CH, kind=f32), sems(2)],
        compiler_params=params,
        cost_estimate=cost(1_000_000_000, 1_000_000),
    )(facts, coords, feat, cot, mask, place_matrix(), weight.T, held(bias.reshape(1, CH)))

    xa, xb, u_inner = lax.optimization_barrier((xa, xb, u_inner))
    left, right, ya, yb = pl.pallas_call(
        edges_kernel,
        out_shape=[shape(4, ROWS, 128)] * 2 + [shape(5, ROWS, 128)] * 2,
        in_specs=[VMEM] * 5,
        out_specs=[VMEM] * 4,
        compiler_params=params,
    )(facts, xa, xb, ylo, yhi)
    u_inner, ya, yb = lax.optimization_barrier((u_inner, ya, yb))
    ya = lax.ppermute(ya, GY, swapped(GY, 0))
    yb = lax.ppermute(yb, GY, swapped(GY, 1))

    windows = window_matrix()
    total = pl.pallas_call(
        gradient_kernel,
        out_shape=shape(GROWS, 128, kind=f32),
        in_specs=[HBM, VMEM, VMEM, HBM],
        out_specs=VMEM,
        scratch_shapes=[
            spot, room(2, 256, 128), room(PLANES, TY + 2, CH, 128), room(slots, GROWS, SPAN), room(slots, 128, SPAN), sems(2)
        ],
        compiler_params=params,
        cost_estimate=cost(2_000_000_000, 1_000_000),
    )(coords, u_inner, middles, windows)
    sums = pl.pallas_call(
        border_kernel,
        out_shape=shape(RED, 128, kind=f32),
        in_specs=[VMEM] * 7,
        out_specs=VMEM,
        scratch_shapes=[room(GROWS, 128, kind=f32)],
        compiler_params=params,
    )(facts, total, left, xlo, ya, yb, ylo)

    def share(parts, copies):
        return pl.pallas_call(
            share_kernel,
            out_shape=shape(copies, chunk, 128, kind=f32),
            in_specs=[VMEM],
            out_specs=VMEM,
            compiler_params=params,
        )(parts)

    n_near, n_far = lax.axis_size(NEAR), lax.axis_size(FAR)
    chunk = RED // n_near
    compact = compact_matrix()
    def convolve(field, field_inner, weights):
        return pl.pallas_call(
            functools.partial(tiles_kernel, field),
            out_shape=shape(slots, CH, 512),
            in_specs=[VMEM, HBM] + [VMEM] * 10,
            out_specs=HBM,
            scratch_shapes=[
                spot, room(PLANES, TY + 2, CH, 128), room(slots, KDIM, SPAN), room(slots, CH, 512), sems(1),
                sems(slots // BATCH),
            ],
            compiler_params=params,
            cost_estimate=cost(200_000_000, 100_000),
        )(facts, coords, field_inner, left, right, ya, yb, windows, live, weights, compact, column)

    part = share(exchange(sums.reshape(n_near, chunk, 128), NEAR), n_far)
    part, left, right = lax.optimization_barrier((part, left, right))
    part = exchange(part, FAR)
    out = convolve(0, u_inner, forward)
    part, out, left, right = lax.optimization_barrier((part, out, left, right))
    total = exchange(share(part, n_near), NEAR).reshape(RED, 128)
    gin = convolve(1, g_inner, backward)
    total, gin = lax.optimization_barrier((total, gin))
    scale = 1.0 / math.sqrt(n_near * n_far * slots * 512)
    grad_weight, grad_bias = pl.pallas_call(
        functools.partial(finish_kernel, scale),
        out_shape=[shape(CH, 3 * KDIM, kind=f32), shape(1, CH, kind=f32)],
        in_specs=[VMEM],
        out_specs=[VMEM] * 2,
        compiler_params=params,
    )(total)
    full_shape = features.shape
    return out.reshape(full_shape), gin.reshape(full_shape), grad_weight.T, grad_bias.reshape(CH)


def solution(mesh):
    fine = Mesh(mesh.devices.reshape(4, 2, 2, 4, 4), ("x", "core", "zl", "y", "zh"))
    spread = (GX, GY, "zh")
    tiles = P(*spread, None, None, None)
    in_specs = (tiles, tiles, P(*spread, None, None), P(*spread, None, None), P(*spread), P(), P())
    out_specs = (tiles, tiles, P(), P())
    return jax.shard_map(local, mesh=fine, in_specs=in_specs, out_specs=out_specs, check_vma=False)
```

```python
import functools
import math

import jax
import jax.numpy as jnp
import numpy as np
from jax import lax
from jax.experimental import pallas as pl
from jax.experimental.pallas import tpu as pltpu
from jax.sharding import Mesh, PartitionSpec as P

TX = 4
TY = 4
CH = 32
ROWS = 2 * CH
PLANES = 8 * TX + 2
SPAN = 10 * 128
KDIM = 9 * CH
GROWS = KDIM + 16
RED = 256
PACK = 216
TAIL = KDIM - PACK
SLOTS = 8
BATCH = 4


def face_matrix():
    m = np.zeros((512, 512), np.float32)
    for u in range(8):
        for c in range(8):
            m[64 * u + c, 16 * u + c] = 1
            m[64 * u + 56 + c, 128 + 16 * u + c] = 1
            m[8 * u + c, 256 + 16 * u + c] = 1
            m[448 + 8 * u + c, 384 + 16 * u + c] = 1
    return jnp.asarray(m, jnp.bfloat16)


def place_matrix():
    m = np.zeros((3, 128, 256), np.float32)
    for h in range(2):
        for b in range(8):
            for c in range(8):
                for tz in range(2):
                    m[tz, 64 * h + 8 * b + c, 128 * h + 16 * b + 8 * tz + c] = 1
                m[2, 64 * h + 8 * b + c, 128 * h + 10 * b + c] = 1
    return jnp.asarray(m, jnp.bfloat16)


def window_matrix():
    m = np.zeros((2, 256, 128), np.float32)
    for tz in range(2):
        for y in range(10):
            for z in range(10):
                gz = 8 * tz - 1 + z
                if gz < 0 or gz > 15:
                    continue
                if y == 0:
                    source = 128 + 112 + gz
                elif y == 9:
                    source = 128 + gz
                else:
                    source = 16 * (y - 1) + gz
                m[tz, source, 10 * y + z] = 1
    return jnp.asarray(m, jnp.bfloat16)


def compact_matrix():
    m = np.zeros((256, 128), np.float32)
    for h in range(2):
        for b in range(8):
            for c in range(8):
                m[128 * h + 10 * b + c, 64 * h + 8 * b + c] = 1
    return jnp.asarray(m, jnp.bfloat16)


def dot(a, b):
    return lax.dot_general(a, b, (((1,), (0,)), ((), ())), preferred_element_type=jnp.float32)


def live_row(mask_ref, facts_ref, slot):
    on = jnp.where(facts_ref[2:3, 0:1] > slot, 1.0, 0.0)
    return mask_ref[slot : slot + 1, :].astype(jnp.float32) * on


def position(coords, slot):
    return coords[0, 0, slot], coords[1, 0, slot], coords[2, 0, slot]


def masked_tiles(facts_ref, feat_ref, cot_ref, mask_ref, slot):
    live = live_row(mask_ref, facts_ref, slot).astype(jnp.bfloat16)
    return jnp.concatenate([feat_ref[slot] * live, cot_ref[slot] * live], axis=0)


def fetch(sems, *pairs):
    copies = [pltpu.make_async_copy(source, target, sems.at[i]) for i, (source, target) in enumerate(pairs)]
    for copy in copies:
        copy.start()
    return copies


def finish_all(copies):
    for copy in copies:
        copy.wait()


def pick(odd, one, other):
    odd = odd.astype(jnp.bfloat16)
    return one * odd + other * (1 - odd)


def faces_kernel(
    facts_ref, coords_hbm, feat_hbm, cot_hbm, mask_hbm, sel_hbm, xa_ref, xb_ref, xlo_ref, ylo_ref, yhi_ref,
    coords, feat_ref, cot_ref, mask_ref, sel_ref, xhi_ref, sems,
):
    copies = fetch(
        sems, (coords_hbm, coords), (feat_hbm, feat_ref), (cot_hbm, cot_ref), (mask_hbm, mask_ref), (sel_hbm, sel_ref)
    )
    for ref in (xlo_ref, xhi_ref, ylo_ref, yhi_ref):
        ref[...] = jnp.zeros_like(ref)
    finish_all(copies)
    tiles = [masked_tiles(facts_ref, feat_ref, cot_ref, mask_ref, slot) for slot in range(SLOTS)]
    found = dot(jnp.concatenate(tiles, axis=0), sel_ref[...])
    for slot in range(SLOTS):
        tx, ty, tz = position(coords, slot)
        sides = ((ylo_ref, tx, ty == 0), (yhi_ref, tx, ty == TY - 1), (xlo_ref, ty, tx == 0), (xhi_ref, ty, tx == TX - 1))
        for block, (ref, place, on) in enumerate(sides):
            part = pltpu.roll(found[ROWS * slot : ROWS * slot + ROWS, 128 * block : 128 * block + 128], 8 * tz, 1)
            part = part * jnp.where(on, 1.0, 0.0)
            ref[place] = ref[place] + part.astype(jnp.bfloat16)
    odd = facts_ref[0:1]
    xa_ref[...] = pick(odd, xlo_ref[...], xhi_ref[...])
    xb_ref[...] = pick(odd, xhi_ref[...], xlo_ref[...])


def edges_kernel(facts_ref, xa_ref, xb_ref, ylo_ref, yhi_ref, left_ref, right_ref, ya_ref, yb_ref):
    odd = facts_ref[0:1]
    left_ref[...] = pick(odd, xa_ref[...], xb_ref[...])
    right_ref[...] = pick(odd, xb_ref[...], xa_ref[...])
    lane = lax.broadcasted_iota(jnp.int32, (ROWS, 128), 1)

    def roll(value, shift):
        return pltpu.roll(value.astype(jnp.float32), shift, 1)

    lo = jnp.where(lane < 16, left_ref[0].astype(jnp.float32), roll(right_ref[0], 16)).astype(jnp.bfloat16)
    hi = jnp.where(lane < 16, roll(left_ref[TY - 1], 16), roll(right_ref[TY - 1], 32)).astype(jnp.bfloat16)
    odd = facts_ref[1:2]
    ya_ref[0:TX] = pick(odd, ylo_ref[...], yhi_ref[...])
    yb_ref[0:TX] = pick(odd, yhi_ref[...], ylo_ref[...])
    ya_ref[TX] = pick(odd, lo, hi)
    yb_ref[TX] = pick(odd, hi, lo)


def turned_weights(weight):
    square = jnp.concatenate([weight, jnp.zeros((CH, 32), jnp.float32)], axis=1).T
    rows = []
    for dx in range(3):
        blocks = [square[CH * (26 - 9 * dx - k) : CH * (27 - 9 * dx - k)] for k in range(9)]
        rows.append(jnp.concatenate(blocks, axis=1))
    return jnp.concatenate(rows, axis=0)


def spread_kernel(
    facts_ref, coords_hbm, feat_ref, cot_ref, mask_ref, place_ref, weight_ref, bias_hbm,
    u_ref, centre_ref, g_ref, live_ref, wf_ref, wb_ref, column_ref,
    coords, bias_ref, sems,
):
    copies = fetch(sems, (coords_hbm, coords), (bias_hbm, bias_ref))
    u_ref[...] = jnp.zeros_like(u_ref)
    g_ref[...] = jnp.zeros_like(g_ref)
    weight = weight_ref[...]
    wf_ref[...] = jnp.concatenate([weight[:, KDIM * dx : KDIM * dx + KDIM] for dx in range(3)], axis=0)
    wb_ref[...] = turned_weights(weight.astype(jnp.float32)).astype(jnp.bfloat16)
    finish_all(copies)
    diagonal = lax.broadcasted_iota(jnp.int32, (CH, CH), 0) == lax.broadcasted_iota(jnp.int32, (CH, CH), 1)
    column = jnp.sum(jnp.where(diagonal, bias_ref[...], 0.0), axis=1, keepdims=True)
    column_ref[...] = jnp.broadcast_to(column, (CH, 128))
    for slot in range(SLOTS):
        tx, ty, tz = position(coords, slot)
        live_ref[slot : slot + 1, :] = live_row(mask_ref, facts_ref, slot)
        tile = masked_tiles(facts_ref, feat_ref, cot_ref, mask_ref, slot)
        stacked = jnp.concatenate([tile[:, 128 * j : 128 * j + 128] for j in range(4)], axis=0)
        spread = dot(stacked, place_ref[tz]).astype(jnp.bfloat16)
        middle = dot(stacked, place_ref[2]).astype(jnp.bfloat16)
        for a in range(8):
            row, col = ROWS * (a // 2), 128 * (a % 2)
            u_ref[8 * tx + a, ty] = u_ref[8 * tx + a, ty] + spread[row : row + CH, col : col + 128]
            g_ref[8 * tx + a, ty] = g_ref[8 * tx + a, ty] + spread[row + CH : row + ROWS, col : col + 128]
            centre_ref[slot, a] = middle[row + CH : row + ROWS, col : col + 128]


def join(field, facts_ref, inner_ref, dense, left_ref, right_ref, ya_ref, yb_ref):
    odd = facts_ref[1:2] > 0.5
    rows = slice(CH * field, CH * field + CH)
    for ty in range(TY):
        dense[1 : PLANES - 1, ty + 1] = inner_ref[:, ty]
        dense[0, ty + 1] = left_ref[ty, rows]
        dense[PLANES - 1, ty + 1] = right_ref[ty, rows]
    for group in range(TX + 1):
        first = ya_ref[group, rows].astype(jnp.float32)
        second = yb_ref[group, rows].astype(jnp.float32)
        lo = jnp.where(odd, first, second)
        hi = jnp.where(odd, second, first)
        for j in range(8 if group < TX else 2):
            plane = 1 + 8 * group + j if group < TX else j * (PLANES - 1)
            dense[plane, 0] = pltpu.roll(lo, (112 - 16 * j) % 128, 1).astype(jnp.bfloat16)
            dense[plane, TY + 1] = pltpu.roll(hi, (128 - 16 * j) % 128, 1).astype(jnp.bfloat16)


def window(coords, slot, dense, window_ref):
    tx, ty, tz = position(coords, slot)
    lane = lax.broadcasted_iota(jnp.int32, (10, CH, 128), 2)
    own = dense[pl.ds(8 * tx, 10), 1 + ty]
    below = dense[pl.ds(8 * tx, 10), ty]
    above = dense[pl.ds(8 * tx, 10), 2 + ty]
    rim = jnp.where(lane >= 112, below, jnp.where(lane < 16, above, jnp.zeros_like(own)))
    both = jnp.concatenate([own.reshape(10 * CH, 128), rim.reshape(10 * CH, 128)], axis=1)
    return dot(both, window_ref[tz])


def fill_columns(windows, columns, slot):
    for k in range(9):
        shift = (k // 3) * 10 + k % 3
        moved = windows if shift == 0 else pltpu.roll(windows, 128 - shift, 1)
        moved = moved.astype(jnp.bfloat16)
        for p in range(10):
            columns[slot, CH * k : CH * k + CH, 128 * p : 128 * p + 128] = moved[CH * p : CH * p + CH]


def gradient_kernel(
    coords_hbm, u_ref, centre_ref, window_hbm, total_ref, coords, window_ref, dense, columns, centre, sems
):
    copies = fetch(sems, (coords_hbm, coords), (window_hbm, window_ref))
    centre[...] = jnp.zeros_like(centre)
    for slot in range(SLOTS):
        columns[slot, KDIM:GROWS, :] = jnp.ones((GROWS - KDIM, SPAN), jnp.bfloat16)
    for plane in (0, PLANES - 1):
        dense[plane] = jnp.zeros((TY + 2, CH, 128), jnp.bfloat16)
    for ty in (0, TY + 1):
        dense[:, ty] = jnp.zeros((PLANES, CH, 128), jnp.bfloat16)
    for ty in range(TY):
        dense[1 : PLANES - 1, ty + 1] = u_ref[:, ty]
    finish_all(copies)
    for slot in range(SLOTS):
        fill_columns(window(coords, slot, dense, window_ref), columns, slot)
        for a in range(8):
            plane = centre_ref[slot, a]
            for dx in range(3):
                centre[slot, CH * dx : CH * dx + CH, 128 * (a + dx) : 128 * (a + dx + 1)] = plane
    products = [dot_nt(columns[slot], centre[slot]) for slot in range(SLOTS)]
    total_ref[...] = sum(products[1:], products[0])


def dot_nt(a, b):
    return lax.dot_general(a, b, (((1,), (1,)), ((), ())), preferred_element_type=jnp.float32)


def face_product(u, g):
    lane = lax.broadcasted_iota(jnp.int32, u.shape, 1)
    z = lane % 16
    width = u.shape[1]
    rows = [jnp.where(z == 0, 0.0, pltpu.roll(u, 1, 1)), u, jnp.where(z == 15, 0.0, pltpu.roll(u, width - 1, 1))]
    level = jnp.where(lane < 128, 0.0, g)
    columns = [pltpu.roll(g, width - 16, 1), level, pltpu.roll(g, 16, 1), jnp.zeros_like(g)]
    return dot_nt(
        jnp.concatenate(rows, axis=0).astype(jnp.bfloat16), jnp.concatenate(columns, axis=0).astype(jnp.bfloat16)
    )


def border_kernel(facts_ref, total_ref, left_ref, xlo_ref, ya_ref, yb_ref, ylo_ref, sums_ref, total):
    odd = facts_ref[1:2] > 0.5
    lane = lax.broadcasted_iota(jnp.int32, (ROWS, 128), 1)
    nothing = jnp.zeros((ROWS, 128), jnp.float32)

    def wide(first, parts):
        return jnp.concatenate([first] + [part.astype(jnp.float32) for part in parts], axis=1)

    def corner(tile):
        return jnp.where(lane >= 112, pltpu.roll(tile.astype(jnp.float32), 112, 1), 0.0)

    low = [jnp.where(odd, ya_ref[i].astype(jnp.float32), yb_ref[i].astype(jnp.float32)) for i in range(TX + 1)]
    x_far = wide(nothing, [left_ref[i] for i in range(TY)])
    x_own = wide(nothing, [xlo_ref[i] for i in range(TY)])
    y_far = wide(corner(low[TX]), low[0:TX])
    y_own = wide(corner(left_ref[0]), [ylo_ref[i] for i in range(TX)])
    third = 3 * CH
    total[...] = total_ref[...]
    total[0:third] += face_product(y_far[0:CH], y_own[CH:ROWS])
    total[2 * third : 3 * third] += face_product(y_own[0:CH], y_far[CH:ROWS])
    column = lax.broadcasted_iota(jnp.int32, (third, 128), 1)
    before = face_product(x_far[0:CH], x_own[CH:ROWS])
    after = face_product(x_own[0:CH], x_far[CH:ROWS])
    for dy in range(3):
        one = jnp.where(column < CH, pltpu.roll(before, (128 - CH * dy) % 128, 1), 0.0)
        two = jnp.where((column >= 2 * CH) & (column < third), pltpu.roll(after, (128 + 2 * CH - CH * dy) % 128, 1), 0.0)
        total[third * dy : third * dy + third] += one + two
    sums_ref[...] = jnp.zeros_like(sums_ref)
    sums_ref[0:PACK, :] = total[0:PACK, :]
    sums_ref[PACK : PACK + 8, :] = total[KDIM : KDIM + 8, :]
    tail = total[PACK:KDIM, :]
    for dx in range(3):
        sums_ref[TAIL * dx : TAIL * dx + TAIL, 96:128] = pltpu.roll(tail, 96 - CH * dx, 1)[:, 96:128]


def cut_kernel(
    facts_ref, coords_hbm, u_ref, g_ref, left_hbm, right_hbm, ya_hbm, yb_hbm, window_hbm, u_cut, g_cut, token_ref,
    coords, left_ref, right_ref, ya_ref, yb_ref, window_ref, u_dense, g_dense, sems,
):
    copies = fetch(
        sems, (coords_hbm, coords), (left_hbm, left_ref), (right_hbm, right_ref), (ya_hbm, ya_ref), (yb_hbm, yb_ref),
        (window_hbm, window_ref),
    )
    token_ref[...] = facts_ref[...]
    finish_all(copies)
    join(0, facts_ref, u_ref, u_dense, left_ref, right_ref, ya_ref, yb_ref)
    join(1, facts_ref, g_ref, g_dense, left_ref, right_ref, ya_ref, yb_ref)
    for slot in range(SLOTS):
        u_cut[slot] = window(coords, slot, u_dense, window_ref).astype(jnp.bfloat16)
        g_cut[slot] = window(coords, slot, g_dense, window_ref).astype(jnp.bfloat16)


def convolve_kernel(
    u_cut, g_cut, column_ref, live, wf_ref, wb_ref, compact_ref, out_hbm, gin_hbm, columns, out_ref, gin_ref, sems
):
    copies = []
    for field, (cut, w_ref, rows_ref, hbm) in enumerate(((u_cut, wf_ref, out_ref, out_hbm), (g_cut, wb_ref, gin_ref, gin_hbm))):
        for slot in range(SLOTS):
            fill_columns(cut[slot].astype(jnp.float32), columns, slot)
            z = dot(w_ref[...], columns[slot])
            y = z[0:CH, 0:1024] + z[CH : 2 * CH, 128:1152] + z[2 * CH : 3 * CH, 256:1280]
            if field == 0:
                y = y + column_ref[:, 0:1]
            y = y.astype(jnp.bfloat16)
            packed = dot(jnp.concatenate([y[:, 256 * j : 256 * j + 256] for j in range(4)], axis=0), compact_ref[...])
            rows = jnp.concatenate([packed[CH * j : CH * j + CH] for j in range(4)], axis=1)
            rows_ref[slot] = (rows * live[slot : slot + 1, :]).astype(jnp.bfloat16)
            if slot % BATCH == BATCH - 1:
                done = pl.ds(slot + 1 - BATCH, BATCH)
                copies.append(pltpu.make_async_copy(rows_ref.at[done], hbm.at[done], sems.at[len(copies)]))
                copies[-1].start()
    finish_all(copies)


def share_kernel(parts_ref, token_ref, out_ref):
    total = parts_ref[0]
    for i in range(1, parts_ref.shape[0]):
        total = total + parts_ref[i]
    for i in range(out_ref.shape[0]):
        out_ref[i] = total


def finish_kernel(scale, sums_ref, weight_ref, bias_ref):
    total = sums_ref[...] * scale
    turned = total.T
    pieces = []
    for dx in range(3):
        pieces.append(turned[CH * dx : CH * dx + CH, 0:PACK])
        pieces.append(turned[96:128, TAIL * dx : TAIL * dx + TAIL])
    weight_ref[...] = jnp.concatenate(pieces, axis=1)
    bias_ref[...] = pltpu.roll(total[PACK : PACK + 8], 128 - CH, 1)[0:1, 0:CH]


def swapped(axis, first):
    count = lax.axis_size(axis)
    pairs = [(i, i + 1) for i in range(first, count - 1, 2)]
    return pairs + [(j, i) for i, j in pairs]


def exchange(block, axes):
    return lax.all_to_all(block, axes, 0, 0, tiled=True)


GX = ("x", "core")
GY = ("zl", "y")
NEAR = ("x", "core", "zl")
FAR = ("y", "zh")
SMEM = pl.BlockSpec(memory_space=pltpu.SMEM)
VMEM = pl.BlockSpec(memory_space=pltpu.VMEM)
HBM = pl.BlockSpec(memory_space=pltpu.HBM)


def local(features, cotangent, masks, coords, counts, weight, bias):
    bf16, f32 = jnp.bfloat16, jnp.float32
    slots = features.shape[3]
    feat = features.reshape(slots, CH, 512)
    cot = cotangent.reshape(slots, CH, 512)
    mask = masks.reshape(slots, 512)
    odd = [lax.axis_index(axis) % 2 for axis in ("core", "y")]
    facts = jnp.stack([*odd, counts.reshape(())]).astype(f32)
    facts = jnp.broadcast_to(jnp.pad(facts, (0, 5))[:, None], (8, 128))
    params = pltpu.CompilerParams(vmem_limit_bytes=24 * 1024 * 1024)

    def shape(*dims, kind=bf16):
        return jax.ShapeDtypeStruct(dims, kind)

    def room(*dims, kind=bf16):
        return pltpu.VMEM(dims, kind)

    def sems(count):
        return pltpu.SemaphoreType.DMA((count,))

    def cost(flops, moved):
        return pl.CostEstimate(flops=flops, bytes_accessed=moved, transcendentals=0)

    def held(x):
        return pltpu.with_memory_space_constraint(x, pltpu.HBM)

    spot = pltpu.SMEM((3, 1, slots), jnp.int32)
    coords = held(coords.reshape(3, 1, slots))
    xa, xb, xlo, ylo, yhi = pl.pallas_call(
        faces_kernel,
        out_shape=[shape(4, ROWS, 128)] * 5,
        in_specs=[VMEM] + [HBM] * 5,
        out_specs=[VMEM] * 5,
        scratch_shapes=[
            spot, room(slots, CH, 512), room(slots, CH, 512), room(slots, 512, kind=jnp.int32), room(512, 512),
            room(4, ROWS, 128), sems(5),
        ],
        compiler_params=params,
    )(facts, coords, held(feat), held(cot), held(mask), held(face_matrix()))
    xb = lax.ppermute(xb, GX, swapped(GX, 1))
    xa = lax.ppermute(xa, GX, swapped(GX, 0))
    inner = shape(PLANES - 2, TY, CH, 128)
    u_inner, middles, g_inner, live, forward, backward, column = pl.pallas_call(
        spread_kernel,
        out_shape=[
            inner, shape(slots, 8, CH, 128), inner, shape(slots, 512, kind=f32), shape(3 * CH, KDIM), shape(3 * CH, KDIM),
            shape(CH, 128, kind=f32),
        ],
        in_specs=[VMEM, HBM] + [VMEM] * 5 + [HBM],
        out_specs=[VMEM] * 7,
        scratch_shapes=[spot, room(1, CH, kind=f32), sems(2)],
        compiler_params=params,
        cost_estimate=cost(1_000_000_000, 1_000_000),
    )(facts, coords, feat, cot, mask, place_matrix(), weight.T, held(bias.reshape(1, CH)))

    xa, xb, u_inner = lax.optimization_barrier((xa, xb, u_inner))
    left, right, ya, yb = pl.pallas_call(
        edges_kernel,
        out_shape=[shape(4, ROWS, 128)] * 2 + [shape(5, ROWS, 128)] * 2,
        in_specs=[VMEM] * 5,
        out_specs=[VMEM] * 4,
        compiler_params=params,
    )(facts, xa, xb, ylo, yhi)
    u_inner, ya, yb = lax.optimization_barrier((u_inner, ya, yb))
    ya = lax.ppermute(ya, GY, swapped(GY, 0))
    yb = lax.ppermute(yb, GY, swapped(GY, 1))

    windows = window_matrix()
    total = pl.pallas_call(
        gradient_kernel,
        out_shape=shape(GROWS, 128, kind=f32),
        in_specs=[HBM, VMEM, VMEM, HBM],
        out_specs=VMEM,
        scratch_shapes=[
            spot, room(2, 256, 128), room(PLANES, TY + 2, CH, 128), room(slots, GROWS, SPAN), room(slots, 128, SPAN), sems(2)
        ],
        compiler_params=params,
        cost_estimate=cost(2_000_000_000, 1_000_000),
    )(coords, u_inner, middles, windows)
    sums = pl.pallas_call(
        border_kernel,
        out_shape=shape(RED, 128, kind=f32),
        in_specs=[VMEM] * 7,
        out_specs=VMEM,
        scratch_shapes=[room(GROWS, 128, kind=f32)],
        compiler_params=params,
    )(facts, total, left, xlo, ya, yb, ylo)

    def share(parts, token, copies):
        return pl.pallas_call(
            share_kernel,
            out_shape=shape(copies, chunk, 128, kind=f32),
            in_specs=[VMEM] * 2,
            out_specs=VMEM,
            compiler_params=params,
        )(parts, token)

    n_near, n_far = lax.axis_size(NEAR), lax.axis_size(FAR)
    chunk = RED // n_near
    compact = compact_matrix()
    part = exchange(sums.reshape(n_near, chunk, 128), NEAR)
    cuts = shape(slots, 10 * CH, 128)
    u_cut, g_cut, token = pl.pallas_call(
        cut_kernel,
        out_shape=[cuts, cuts, shape(8, 128, kind=f32)],
        in_specs=[VMEM, HBM, VMEM, VMEM] + [HBM] * 5,
        out_specs=[VMEM] * 3,
        scratch_shapes=[
            spot, room(4, ROWS, 128), room(4, ROWS, 128), room(5, ROWS, 128), room(5, ROWS, 128), room(2, 256, 128),
            room(PLANES, TY + 2, CH, 128), room(PLANES, TY + 2, CH, 128), sems(6),
        ],
        compiler_params=params,
        cost_estimate=cost(200_000_000, 100_000),
    )(facts, coords, u_inner, g_inner, held(left), held(right), held(ya), held(yb), held(windows))
    part = exchange(share(part, token, n_far), FAR)
    rows = shape(slots, CH, 512)
    out, gin = pl.pallas_call(
        convolve_kernel,
        out_shape=[rows, rows],
        in_specs=[VMEM] * 7,
        out_specs=[HBM] * 2,
        scratch_shapes=[
            room(slots, KDIM, SPAN), room(slots, CH, 512), room(slots, CH, 512), sems(2 * slots // BATCH)
        ],
        compiler_params=params,
        cost_estimate=cost(200_000_000, 100_000),
    )(u_cut, g_cut, column, live, forward, backward, compact)
    part, out, gin = lax.optimization_barrier((part, out, gin))
    total = exchange(share(part, facts, n_near), NEAR).reshape(RED, 128)
    scale = 1.0 / math.sqrt(n_near * n_far * slots * 512)
    grad_weight, grad_bias = pl.pallas_call(
        functools.partial(finish_kernel, scale),
        out_shape=[shape(CH, 3 * KDIM, kind=f32), shape(1, CH, kind=f32)],
        in_specs=[VMEM],
        out_specs=[VMEM] * 2,
        compiler_params=params,
    )(total)
    full_shape = features.shape
    return out.reshape(full_shape), gin.reshape(full_shape), grad_weight.T, grad_bias.reshape(CH)


def solution(mesh):
    fine = Mesh(mesh.devices.reshape(4, 2, 2, 4, 4), ("x", "core", "zl", "y", "zh"))
    spread = (GX, GY, "zh")
    tiles = P(*spread, None, None, None)
    in_specs = (tiles, tiles, P(*spread, None, None), P(*spread, None, None), P(*spread), P(), P())
    out_specs = (tiles, tiles, P(), P())
    return jax.shard_map(local, mesh=fine, in_specs=in_specs, out_specs=out_specs, check_vma=False)
```

```python
import functools
import math

import jax
import jax.numpy as jnp
import numpy as np
from jax import lax
from jax.experimental import pallas as pl
from jax.experimental.pallas import tpu as pltpu
from jax.sharding import Mesh, PartitionSpec as P

TX = 4
TY = 4
CH = 32
ROWS = 2 * CH
PLANES = 8 * TX + 2
SPAN = 10 * 128
KDIM = 9 * CH
GROWS = KDIM + 16
RED = 256
PACK = 216
TAIL = KDIM - PACK
SLOTS = 8
BATCH = 4


def face_matrix():
    m = np.zeros((512, 512), np.float32)
    for u in range(8):
        for c in range(8):
            m[64 * u + c, 16 * u + c] = 1
            m[64 * u + 56 + c, 128 + 16 * u + c] = 1
            m[8 * u + c, 256 + 16 * u + c] = 1
            m[448 + 8 * u + c, 384 + 16 * u + c] = 1
    return jnp.asarray(m, jnp.bfloat16)


def place_matrix():
    m = np.zeros((3, 128, 256), np.float32)
    for h in range(2):
        for b in range(8):
            for c in range(8):
                for tz in range(2):
                    m[tz, 64 * h + 8 * b + c, 128 * h + 16 * b + 8 * tz + c] = 1
                m[2, 64 * h + 8 * b + c, 128 * h + 10 * b + c] = 1
    return jnp.asarray(m, jnp.bfloat16)


def window_matrix():
    m = np.zeros((2, 256, 128), np.float32)
    for tz in range(2):
        for y in range(10):
            for z in range(10):
                gz = 8 * tz - 1 + z
                if gz < 0 or gz > 15:
                    continue
                if y == 0:
                    source = 128 + 112 + gz
                elif y == 9:
                    source = 128 + gz
                else:
                    source = 16 * (y - 1) + gz
                m[tz, source, 10 * y + z] = 1
    return jnp.asarray(m, jnp.bfloat16)


def compact_matrix():
    m = np.zeros((256, 128), np.float32)
    for h in range(2):
        for b in range(8):
            for c in range(8):
                m[128 * h + 10 * b + c, 64 * h + 8 * b + c] = 1
    return jnp.asarray(m, jnp.bfloat16)


def dot(a, b):
    return lax.dot_general(a, b, (((1,), (0,)), ((), ())), preferred_element_type=jnp.float32)


def live_row(mask_ref, facts_ref, slot):
    on = jnp.where(facts_ref[2:3, 0:1] > slot, 1.0, 0.0)
    return mask_ref[slot : slot + 1, :].astype(jnp.float32) * on


def position(coords, slot):
    return coords[0, 0, slot], coords[1, 0, slot], coords[2, 0, slot]


def masked_tiles(facts_ref, feat_ref, cot_ref, mask_ref, slot):
    live = live_row(mask_ref, facts_ref, slot).astype(jnp.bfloat16)
    return jnp.concatenate([feat_ref[slot] * live, cot_ref[slot] * live], axis=0)


def fetch(sems, *pairs):
    copies = [pltpu.make_async_copy(source, target, sems.at[i]) for i, (source, target) in enumerate(pairs)]
    for copy in copies:
        copy.start()
    return copies


def finish_all(copies):
    for copy in copies:
        copy.wait()


def pick(odd, one, other):
    odd = odd.astype(jnp.bfloat16)
    return one * odd + other * (1 - odd)


def faces_kernel(
    facts_ref, coords_hbm, feat_hbm, cot_hbm, mask_hbm, sel_hbm, xa_ref, xb_ref, xlo_ref, ylo_ref, yhi_ref,
    coords, feat_ref, cot_ref, mask_ref, sel_ref, xhi_ref, sems,
):
    copies = fetch(
        sems, (coords_hbm, coords), (feat_hbm, feat_ref), (cot_hbm, cot_ref), (mask_hbm, mask_ref), (sel_hbm, sel_ref)
    )
    for ref in (xlo_ref, xhi_ref, ylo_ref, yhi_ref):
        ref[...] = jnp.zeros_like(ref)
    finish_all(copies)
    tiles = [masked_tiles(facts_ref, feat_ref, cot_ref, mask_ref, slot) for slot in range(SLOTS)]
    found = dot(jnp.concatenate(tiles, axis=0), sel_ref[...])
    for slot in range(SLOTS):
        tx, ty, tz = position(coords, slot)
        sides = ((ylo_ref, tx, ty == 0), (yhi_ref, tx, ty == TY - 1), (xlo_ref, ty, tx == 0), (xhi_ref, ty, tx == TX - 1))
        for block, (ref, place, on) in enumerate(sides):
            part = pltpu.roll(found[ROWS * slot : ROWS * slot + ROWS, 128 * block : 128 * block + 128], 8 * tz, 1)
            part = part * jnp.where(on, 1.0, 0.0)
            ref[place] = ref[place] + part.astype(jnp.bfloat16)
    odd = facts_ref[0:1]
    xa_ref[...] = pick(odd, xlo_ref[...], xhi_ref[...])
    xb_ref[...] = pick(odd, xhi_ref[...], xlo_ref[...])


def edges_kernel(facts_ref, xa_ref, xb_ref, ylo_ref, yhi_ref, left_ref, right_ref, ya_ref, yb_ref):
    odd = facts_ref[0:1]
    left_ref[...] = pick(odd, xa_ref[...], xb_ref[...])
    right_ref[...] = pick(odd, xb_ref[...], xa_ref[...])
    lane = lax.broadcasted_iota(jnp.int32, (ROWS, 128), 1)

    def roll(value, shift):
        return pltpu.roll(value.astype(jnp.float32), shift, 1)

    lo = jnp.where(lane < 16, left_ref[0].astype(jnp.float32), roll(right_ref[0], 16)).astype(jnp.bfloat16)
    hi = jnp.where(lane < 16, roll(left_ref[TY - 1], 16), roll(right_ref[TY - 1], 32)).astype(jnp.bfloat16)
    odd = facts_ref[1:2]
    ya_ref[0:TX] = pick(odd, ylo_ref[...], yhi_ref[...])
    yb_ref[0:TX] = pick(odd, yhi_ref[...], ylo_ref[...])
    ya_ref[TX] = pick(odd, lo, hi)
    yb_ref[TX] = pick(odd, hi, lo)


def turned_weights(weight):
    square = jnp.concatenate([weight, jnp.zeros((CH, 32), jnp.float32)], axis=1).T
    rows = []
    for dx in range(3):
        blocks = [square[CH * (26 - 9 * dx - k) : CH * (27 - 9 * dx - k)] for k in range(9)]
        rows.append(jnp.concatenate(blocks, axis=1))
    return jnp.concatenate(rows, axis=0)


def spread_kernel(
    facts_ref, coords_hbm, feat_ref, cot_ref, mask_ref, place_ref, weight_ref, bias_hbm,
    u_ref, centre_ref, g_ref, live_ref, wf_ref, wb_ref, column_ref,
    coords, bias_ref, sems,
):
    copies = fetch(sems, (coords_hbm, coords), (bias_hbm, bias_ref))
    u_ref[...] = jnp.zeros_like(u_ref)
    g_ref[...] = jnp.zeros_like(g_ref)
    weight = weight_ref[...]
    wf_ref[...] = jnp.concatenate([weight[:, KDIM * dx : KDIM * dx + KDIM] for dx in range(3)], axis=0)
    wb_ref[...] = turned_weights(weight.astype(jnp.float32)).astype(jnp.bfloat16)
    finish_all(copies)
    diagonal = lax.broadcasted_iota(jnp.int32, (CH, CH), 0) == lax.broadcasted_iota(jnp.int32, (CH, CH), 1)
    column = jnp.sum(jnp.where(diagonal, bias_ref[...], 0.0), axis=1, keepdims=True)
    column_ref[...] = jnp.broadcast_to(column, (CH, 128))
    for slot in range(SLOTS):
        tx, ty, tz = position(coords, slot)
        live_ref[slot : slot + 1, :] = live_row(mask_ref, facts_ref, slot)
        tile = masked_tiles(facts_ref, feat_ref, cot_ref, mask_ref, slot)
        stacked = jnp.concatenate([tile[:, 128 * j : 128 * j + 128] for j in range(4)], axis=0)
        spread = dot(stacked, place_ref[tz]).astype(jnp.bfloat16)
        middle = dot(stacked, place_ref[2]).astype(jnp.bfloat16)
        for a in range(8):
            row, col = ROWS * (a // 2), 128 * (a % 2)
            u_ref[8 * tx + a, ty] = u_ref[8 * tx + a, ty] + spread[row : row + CH, col : col + 128]
            g_ref[8 * tx + a, ty] = g_ref[8 * tx + a, ty] + spread[row + CH : row + ROWS, col : col + 128]
            centre_ref[slot, a] = middle[row + CH : row + ROWS, col : col + 128]


def join(field, facts_ref, inner_ref, dense, left_ref, right_ref, ya_ref, yb_ref):
    odd = facts_ref[1:2] > 0.5
    rows = slice(CH * field, CH * field + CH)
    for ty in range(TY):
        dense[1 : PLANES - 1, ty + 1] = inner_ref[:, ty]
        dense[0, ty + 1] = left_ref[ty, rows]
        dense[PLANES - 1, ty + 1] = right_ref[ty, rows]
    for group in range(TX + 1):
        first = ya_ref[group, rows].astype(jnp.float32)
        second = yb_ref[group, rows].astype(jnp.float32)
        lo = jnp.where(odd, first, second)
        hi = jnp.where(odd, second, first)
        for j in range(8 if group < TX else 2):
            plane = 1 + 8 * group + j if group < TX else j * (PLANES - 1)
            dense[plane, 0] = pltpu.roll(lo, (112 - 16 * j) % 128, 1).astype(jnp.bfloat16)
            dense[plane, TY + 1] = pltpu.roll(hi, (128 - 16 * j) % 128, 1).astype(jnp.bfloat16)


def window(coords, slot, dense, window_ref):
    tx, ty, tz = position(coords, slot)
    lane = lax.broadcasted_iota(jnp.int32, (10, CH, 128), 2)
    own = dense[pl.ds(8 * tx, 10), 1 + ty]
    below = dense[pl.ds(8 * tx, 10), ty]
    above = dense[pl.ds(8 * tx, 10), 2 + ty]
    rim = jnp.where(lane >= 112, below, jnp.where(lane < 16, above, jnp.zeros_like(own)))
    both = jnp.concatenate([own.reshape(10 * CH, 128), rim.reshape(10 * CH, 128)], axis=1)
    return dot(both, window_ref[tz])


def fill_columns(windows, columns, slot):
    for k in range(9):
        shift = (k // 3) * 10 + k % 3
        moved = windows if shift == 0 else pltpu.roll(windows, 128 - shift, 1)
        moved = moved.astype(jnp.bfloat16)
        for p in range(10):
            columns[slot, CH * k : CH * k + CH, 128 * p : 128 * p + 128] = moved[CH * p : CH * p + CH]


def gradient_kernel(
    coords_hbm, u_ref, centre_ref, window_hbm, total_ref, coords, window_ref, dense, columns, centre, sems
):
    copies = fetch(sems, (coords_hbm, coords), (window_hbm, window_ref))
    centre[...] = jnp.zeros_like(centre)
    for slot in range(SLOTS):
        columns[slot, KDIM:GROWS, :] = jnp.ones((GROWS - KDIM, SPAN), jnp.bfloat16)
    for plane in (0, PLANES - 1):
        dense[plane] = jnp.zeros((TY + 2, CH, 128), jnp.bfloat16)
    for ty in (0, TY + 1):
        dense[:, ty] = jnp.zeros((PLANES, CH, 128), jnp.bfloat16)
    for ty in range(TY):
        dense[1 : PLANES - 1, ty + 1] = u_ref[:, ty]
    finish_all(copies)
    for slot in range(SLOTS):
        fill_columns(window(coords, slot, dense, window_ref), columns, slot)
        for a in range(8):
            plane = centre_ref[slot, a]
            for dx in range(3):
                centre[slot, CH * dx : CH * dx + CH, 128 * (a + dx) : 128 * (a + dx + 1)] = plane
    products = [dot_nt(columns[slot], centre[slot]) for slot in range(SLOTS)]
    total_ref[...] = sum(products[1:], products[0])


def dot_nt(a, b):
    return lax.dot_general(a, b, (((1,), (1,)), ((), ())), preferred_element_type=jnp.float32)


def face_product(u, g):
    lane = lax.broadcasted_iota(jnp.int32, u.shape, 1)
    z = lane % 16
    width = u.shape[1]
    rows = [jnp.where(z == 0, 0.0, pltpu.roll(u, 1, 1)), u, jnp.where(z == 15, 0.0, pltpu.roll(u, width - 1, 1))]
    level = jnp.where(lane < 128, 0.0, g)
    columns = [pltpu.roll(g, width - 16, 1), level, pltpu.roll(g, 16, 1), jnp.zeros_like(g)]
    return dot_nt(
        jnp.concatenate(rows, axis=0).astype(jnp.bfloat16), jnp.concatenate(columns, axis=0).astype(jnp.bfloat16)
    )


def border_kernel(facts_ref, total_ref, left_ref, xlo_ref, ya_ref, yb_ref, ylo_ref, sums_ref, total):
    odd = facts_ref[1:2] > 0.5
    lane = lax.broadcasted_iota(jnp.int32, (ROWS, 128), 1)
    nothing = jnp.zeros((ROWS, 128), jnp.float32)

    def wide(first, parts):
        return jnp.concatenate([first] + [part.astype(jnp.float32) for part in parts], axis=1)

    def corner(tile):
        return jnp.where(lane >= 112, pltpu.roll(tile.astype(jnp.float32), 112, 1), 0.0)

    low = [jnp.where(odd, ya_ref[i].astype(jnp.float32), yb_ref[i].astype(jnp.float32)) for i in range(TX + 1)]
    x_far = wide(nothing, [left_ref[i] for i in range(TY)])
    x_own = wide(nothing, [xlo_ref[i] for i in range(TY)])
    y_far = wide(corner(low[TX]), low[0:TX])
    y_own = wide(corner(left_ref[0]), [ylo_ref[i] for i in range(TX)])
    third = 3 * CH
    total[...] = total_ref[...]
    total[0:third] += face_product(y_far[0:CH], y_own[CH:ROWS])
    total[2 * third : 3 * third] += face_product(y_own[0:CH], y_far[CH:ROWS])
    column = lax.broadcasted_iota(jnp.int32, (third, 128), 1)
    before = face_product(x_far[0:CH], x_own[CH:ROWS])
    after = face_product(x_own[0:CH], x_far[CH:ROWS])
    for dy in range(3):
        one = jnp.where(column < CH, pltpu.roll(before, (128 - CH * dy) % 128, 1), 0.0)
        two = jnp.where((column >= 2 * CH) & (column < third), pltpu.roll(after, (128 + 2 * CH - CH * dy) % 128, 1), 0.0)
        total[third * dy : third * dy + third] += one + two
    sums_ref[...] = jnp.zeros_like(sums_ref)
    sums_ref[0:PACK, :] = total[0:PACK, :]
    sums_ref[PACK : PACK + 8, :] = total[KDIM : KDIM + 8, :]
    tail = total[PACK:KDIM, :]
    for dx in range(3):
        sums_ref[TAIL * dx : TAIL * dx + TAIL, 96:128] = pltpu.roll(tail, 96 - CH * dx, 1)[:, 96:128]


def convolve_tiles(window_of, column_ref, live, w_ref, compact_ref, out_hbm, columns, out_ref, sems):
    copies = []
    for slot in range(SLOTS):
        fill_columns(window_of(slot), columns, slot)
        z = dot(w_ref[...], columns[slot])
        y = z[0:CH, 0:1024] + z[CH : 2 * CH, 128:1152] + z[2 * CH : 3 * CH, 256:1280]
        if column_ref is not None:
            y = y + column_ref[:, 0:1]
        y = y.astype(jnp.bfloat16)
        packed = dot(jnp.concatenate([y[:, 256 * j : 256 * j + 256] for j in range(4)], axis=0), compact_ref[...])
        rows = jnp.concatenate([packed[CH * j : CH * j + CH] for j in range(4)], axis=1)
        out_ref[slot] = (rows * live[slot : slot + 1, :]).astype(jnp.bfloat16)
        if slot % BATCH == BATCH - 1:
            done = pl.ds(slot + 1 - BATCH, BATCH)
            copies.append(pltpu.make_async_copy(out_ref.at[done], out_hbm.at[done], sems.at[slot // BATCH]))
            copies[-1].start()
    finish_all(copies)


def tiles_kernel(
    field, facts_ref, coords_hbm, inner_ref, left_ref, right_ref, ya_ref, yb_ref, window_ref, live, w_ref, compact_ref, column_ref,
    out_hbm, coords, dense, columns, out_ref, start_sems, sems,
):
    copies = fetch(start_sems, (coords_hbm, coords))
    join(field, facts_ref, inner_ref, dense, left_ref, right_ref, ya_ref, yb_ref)
    finish_all(copies)
    convolve_tiles(
        lambda slot: window(coords, slot, dense, window_ref), column_ref if field == 0 else None, live, w_ref, compact_ref,
        out_hbm, columns, out_ref, sems,
    )


def share_kernel(parts_ref, out_ref):
    total = parts_ref[0]
    for i in range(1, parts_ref.shape[0]):
        total = total + parts_ref[i]
    for i in range(out_ref.shape[0]):
        out_ref[i] = total


def finish_kernel(scale, sums_ref, weight_ref, bias_ref):
    total = sums_ref[...] * scale
    turned = total.T
    pieces = []
    for dx in range(3):
        pieces.append(turned[CH * dx : CH * dx + CH, 0:PACK])
        pieces.append(turned[96:128, TAIL * dx : TAIL * dx + TAIL])
    weight_ref[...] = jnp.concatenate(pieces, axis=1)
    bias_ref[...] = pltpu.roll(total[PACK : PACK + 8], 128 - CH, 1)[0:1, 0:CH]


def swapped(axis, first):
    count = lax.axis_size(axis)
    pairs = [(i, i + 1) for i in range(first, count - 1, 2)]
    return pairs + [(j, i) for i, j in pairs]


def exchange(block, axes):
    return lax.all_to_all(block, axes, 0, 0, tiled=True)


GX = ("x", "core")
GY = ("zl", "y")
NEAR = ("core", "zl", "y")
FAR = ("x", "zh")
SMEM = pl.BlockSpec(memory_space=pltpu.SMEM)
VMEM = pl.BlockSpec(memory_space=pltpu.VMEM)
HBM = pl.BlockSpec(memory_space=pltpu.HBM)


def local(features, cotangent, masks, coords, counts, weight, bias):
    bf16, f32 = jnp.bfloat16, jnp.float32
    slots = features.shape[3]
    feat = features.reshape(slots, CH, 512)
    cot = cotangent.reshape(slots, CH, 512)
    mask = masks.reshape(slots, 512)
    odd = [lax.axis_index(axis) % 2 for axis in ("core", "y")]
    facts = jnp.stack([*odd, counts.reshape(())]).astype(f32)
    facts = jnp.broadcast_to(jnp.pad(facts, (0, 5))[:, None], (8, 128))
    params = pltpu.CompilerParams(vmem_limit_bytes=24 * 1024 * 1024)

    def shape(*dims, kind=bf16):
        return jax.ShapeDtypeStruct(dims, kind)

    def room(*dims, kind=bf16):
        return pltpu.VMEM(dims, kind)

    def sems(count):
        return pltpu.SemaphoreType.DMA((count,))

    def cost(flops, moved):
        return pl.CostEstimate(flops=flops, bytes_accessed=moved, transcendentals=0)

    def held(x):
        return pltpu.with_memory_space_constraint(x, pltpu.HBM)

    spot = pltpu.SMEM((3, 1, slots), jnp.int32)
    coords = held(coords.reshape(3, 1, slots))
    xa, xb, xlo, ylo, yhi = pl.pallas_call(
        faces_kernel,
        out_shape=[shape(4, ROWS, 128)] * 5,
        in_specs=[VMEM] + [HBM] * 5,
        out_specs=[VMEM] * 5,
        scratch_shapes=[
            spot, room(slots, CH, 512), room(slots, CH, 512), room(slots, 512, kind=jnp.int32), room(512, 512),
            room(4, ROWS, 128), sems(5),
        ],
        compiler_params=params,
    )(facts, coords, held(feat), held(cot), held(mask), held(face_matrix()))
    xb = lax.ppermute(xb, GX, swapped(GX, 1))
    xa = lax.ppermute(xa, GX, swapped(GX, 0))
    inner = shape(PLANES - 2, TY, CH, 128)
    u_inner, middles, g_inner, live, forward, backward, column = pl.pallas_call(
        spread_kernel,
        out_shape=[
            inner, shape(slots, 8, CH, 128), inner, shape(slots, 512, kind=f32), shape(3 * CH, KDIM), shape(3 * CH, KDIM),
            shape(CH, 128, kind=f32),
        ],
        in_specs=[VMEM, HBM] + [VMEM] * 5 + [HBM],
        out_specs=[VMEM] * 7,
        scratch_shapes=[spot, room(1, CH, kind=f32), sems(2)],
        compiler_params=params,
        cost_estimate=cost(1_000_000_000, 1_000_000),
    )(facts, coords, feat, cot, mask, place_matrix(), weight.T, held(bias.reshape(1, CH)))

    xa, xb, u_inner = lax.optimization_barrier((xa, xb, u_inner))
    left, right, ya, yb = pl.pallas_call(
        edges_kernel,
        out_shape=[shape(4, ROWS, 128)] * 2 + [shape(5, ROWS, 128)] * 2,
        in_specs=[VMEM] * 5,
        out_specs=[VMEM] * 4,
        compiler_params=params,
    )(facts, xa, xb, ylo, yhi)
    u_inner, ya, yb = lax.optimization_barrier((u_inner, ya, yb))
    ya = lax.ppermute(ya, GY, swapped(GY, 0))
    yb = lax.ppermute(yb, GY, swapped(GY, 1))

    windows = window_matrix()
    total = pl.pallas_call(
        gradient_kernel,
        out_shape=shape(GROWS, 128, kind=f32),
        in_specs=[HBM, VMEM, VMEM, HBM],
        out_specs=VMEM,
        scratch_shapes=[
            spot, room(2, 256, 128), room(PLANES, TY + 2, CH, 128), room(slots, GROWS, SPAN), room(slots, 128, SPAN), sems(2)
        ],
        compiler_params=params,
        cost_estimate=cost(2_000_000_000, 1_000_000),
    )(coords, u_inner, middles, windows)
    sums = pl.pallas_call(
        border_kernel,
        out_shape=shape(RED, 128, kind=f32),
        in_specs=[VMEM] * 7,
        out_specs=VMEM,
        scratch_shapes=[room(GROWS, 128, kind=f32)],
        compiler_params=params,
    )(facts, total, left, xlo, ya, yb, ylo)

    def share(parts, copies):
        return pl.pallas_call(
            share_kernel,
            out_shape=shape(copies, chunk, 128, kind=f32),
            in_specs=[VMEM],
            out_specs=VMEM,
            compiler_params=params,
        )(parts)

    n_near, n_far = lax.axis_size(NEAR), lax.axis_size(FAR)
    chunk = RED // n_near
    compact = compact_matrix()
    def convolve(field, field_inner, weights):
        return pl.pallas_call(
            functools.partial(tiles_kernel, field),
            out_shape=shape(slots, CH, 512),
            in_specs=[VMEM, HBM] + [VMEM] * 10,
            out_specs=HBM,
            scratch_shapes=[
                spot, room(PLANES, TY + 2, CH, 128), room(slots, KDIM, SPAN), room(slots, CH, 512), sems(1),
                sems(slots // BATCH),
            ],
            compiler_params=params,
            cost_estimate=cost(200_000_000, 100_000),
        )(facts, coords, field_inner, left, right, ya, yb, windows, live, weights, compact, column)

    part = share(exchange(sums.reshape(n_near, chunk, 128), NEAR), n_far)
    part, left, right = lax.optimization_barrier((part, left, right))
    part = exchange(part, FAR)
    out = convolve(0, u_inner, forward)
    part, out, left, right = lax.optimization_barrier((part, out, left, right))
    total = exchange(share(part, n_near), NEAR).reshape(RED, 128)
    gin = convolve(1, g_inner, backward)
    total, gin = lax.optimization_barrier((total, gin))
    scale = 1.0 / math.sqrt(n_near * n_far * slots * 512)
    grad_weight, grad_bias = pl.pallas_call(
        functools.partial(finish_kernel, scale),
        out_shape=[shape(CH, 3 * KDIM, kind=f32), shape(1, CH, kind=f32)],
        in_specs=[VMEM],
        out_specs=[VMEM] * 2,
        compiler_params=params,
    )(total)
    full_shape = features.shape
    return out.reshape(full_shape), gin.reshape(full_shape), grad_weight.T, grad_bias.reshape(CH)


def solution(mesh):
    fine = Mesh(mesh.devices.reshape(4, 2, 2, 4, 4), ("x", "core", "zl", "y", "zh"))
    spread = (GX, GY, "zh")
    tiles = P(*spread, None, None, None)
    in_specs = (tiles, tiles, P(*spread, None, None), P(*spread, None, None), P(*spread), P(), P())
    out_specs = (tiles, tiles, P(), P())
    return jax.shard_map(local, mesh=fine, in_specs=in_specs, out_specs=out_specs, check_vma=False)
```
